256 devices in a mesh: group: 8 (over z), shard: 32 (over x, y, core).
Axes of the slice: x: 4, y: 4, z: 8, core: 2. Of those that a mesh axis runs over, the one named last changes fastest.
Arguments:
- offer_attribute_matrix: bfloat16 [1024, 128, 1024], P(('group', 'shard')), may hold values from -6 to 6
- kept_offers: int32 [1024, 32], P(('group', 'shard')), may hold values from 0 to 127, as said below
- expert_target: int32 [1024, 6], P(('group', 'shard')), may hold values from 0 to 31, all different within a row; in each aligned block of 4 rows (0 to 3, 4 to 7, ...) at most 2 rows name the same one
- sequence_extent: int32 [1024], P(('group', 'shard')), may hold values from 1 to 128
- behaviour_sequence: bfloat16 [1024, 128, 512], P(('group', 'shard')), may hold values from -6 to 6
- inner_projection_matrix: bfloat16 [1024, 1024], replicated, may hold values from -0.1875 to 0.1875
- student_rating_vector: bfloat16 [1024], replicated, may hold values from -0.1875 to 0.1875
- asking_matrix: bfloat16 [32, 1024, 512], P('shard'), may hold values from -0.1875 to 0.1875
- lookup_matrix: bfloat16 [32, 512, 512], P('shard'), may hold values from -0.25 to 0.25
- content_matrix: bfloat16 [32, 512, 512], P('shard'), may hold values from -0.25 to 0.25
- expert_rating_vector: bfloat16 [32, 512], P('shard'), may hold values from -1.1953125 to 1.1953125
Outputs:
- grad_hidden: float32 [1024, 1024], P('shard')
- grad_score: float32 [1024], replicated
The draws below stay inside these ranges and needn't reach their ends.
Inputs may be any that keep to these rules, and one draw needn't show every extreme that they name: `kept_offers`: the 32 survivors of a request are distinct candidates. `expert_target`: each request names 6 distinct experts; the requests of one device name any expert at most 2 times, a bound that some block reaches.
All inputs are finite; a program needn't handle non-finite values.
Results may differ from the reference program's by a relative error of at most 0.005.
Values may be sent and summed in bfloat16 or wider, within the bound.
A program may use at most 128 MiB of HBM per device.

```python
import math
import jax
import jax.numpy as jnp
import numpy as np
from jax import lax

DP = 1024
HP = 1024
ATTENDER_GANGS = 8
DA = 512
CAND = 128
KS = 32
HLEN = 128
TOPR = 6
REQ_DEV = 4
REQUESTS = 1024
EXPERTS = 32
CAP = 2
N_GROUP = 8
N_SHARD = 32


def draw_kept_offers(key, part):
    row_keys = jax.random.split(jax.random.fold_in(key, 17), REQUESTS)

    def one_row(row_key):
        return jax.random.permutation(row_key, CAND)[:KS]
    return jax.vmap(one_row)(row_keys).astype(jnp.int32)


def place_ends(entries, stream_key, least, top_value):
    longest = entries.shape.index(max(entries.shape))
    spots = []
    for shift in (0, 1):
        where = [jax.random.randint(jax.random.fold_in(stream_key, axis), (), 0, length) for axis, length in enumerate(entries.shape)]
        where[longest] = (where[longest] + shift) % entries.shape[longest]
        spots.append(tuple(where))
    return entries.at[spots[0]].set(least).at[spots[1]].set(top_value)


def levels(own_key, shape, pieces, least, top_value):
    def one(position, parts):
        heights = jax.random.uniform(jax.random.fold_in(jax.random.fold_in(own_key, 6), position), (parts,), jnp.float32, least / len(pieces), top_value / len(pieces))
        return jnp.repeat(jnp.exp(heights), shape[position] // parts).reshape((-1,) + (1,) * (len(shape) - position - 1))

    level = one(*pieces[0])
    for cut in pieces[1:]:
        level = level * one(*cut)
    return level


def shared_out(own_key, own, number, rows, amount, top, limit, skew):
    sequence = jax.random.permutation(own_key, amount)
    crowded, ordinary = portions_of(amount, rows * top, limit, skew, True), portions_of(amount, rows * top, limit, skew, False)
    places = jnp.arange(amount)

    def named(sizes, rotation):
        used = int((sizes > 0).sum())
        fixed = max(1, used // 4)
        shifted = fixed + (places - fixed + rotation * (used - fixed)) % max(1, amount - fixed)
        return jnp.zeros((amount,), jnp.int32).at[sequence[jnp.where(places < fixed, places, shifted)]].set(jnp.asarray(sizes, jnp.int32))

    sizes = jnp.where(number % 4 == 0, named(crowded, number // 4), named(ordinary, number - number // 4 - 1))
    mixed = jax.random.permutation(jax.random.fold_in(own, 3), amount)
    donor, sink = mixed[0:amount // 2 * 2:2], mixed[1:amount // 2 * 2:2]
    slack = jnp.minimum(sizes[donor] - 1, limit - sizes[sink]) // 2
    slack = jnp.where((donor == sequence[0]) | (sink == sequence[0]) | (sizes[sink] == 0), 0, jnp.maximum(slack, 0))
    shifted = jax.random.randint(jax.random.fold_in(own, 4), (amount // 2,), 0, 1 << 20) % (slack + 1)
    sizes = sizes.at[donor].add(-shifted).at[sink].add(shifted)
    labels = jnp.searchsorted(jnp.cumsum(sizes), jnp.arange(rows * top), side="right").astype(jnp.int32)
    listing = labels.reshape(top, rows).T
    listing = listing[jax.random.permutation(jax.random.fold_in(own, 1), rows)]
    rotation = jax.random.randint(jax.random.fold_in(own, 2), (rows, 1), 0, top)
    return jnp.take_along_axis(listing, (jnp.arange(top)[None, :] + rotation) % top, axis=1)


def portions_of(amount, total, bound, skew, full):
    portions = [(1 << 20) // math.isqrt(grade ** skew) + 1 for grade in range(1, amount + 1)]
    largest = bound if full else min(bound, max(-(-total // amount), total * portions[0] // sum(portions)))
    least = 1 if total - largest >= amount - 1 else 0
    holding, surplus = [largest] + [least] * (amount - 1), total - largest - least * (amount - 1)
    while surplus > 0:
        movable = [i for i in range(1, amount) if holding[i] < largest] or [i for i in range(1, amount) if holding[i] < bound]
        pool, budget = sum([portions[i] for i in movable]), surplus
        for i in movable:
            addition = min(bound - holding[i], max(1, budget * portions[i] // pool), surplus)
            holding[i] = holding[i] + addition
            surplus = surplus - addition
    return np.array(holding)


def centred(own_key, dims, width, reach, cuts=(), held_as=jnp.bfloat16):
    gain = levels(own_key, dims, cuts, -0.22, 0.18) if cuts else 1.0
    drawn = jax.random.normal(own_key, dims, jnp.float32) * width * gain
    return jnp.minimum(jnp.maximum(drawn, -reach), reach).astype(held_as)


def setup_inputs(seed: int = 0) -> dict:
    key_of = jax.random.split(jax.random.key(seed), 12)
    offer_attribute_matrix = centred(key_of[0], (REQUESTS, CAND, DP), 1.0, 6.0, ((0, 256),))
    kept_offers = draw_kept_offers(jax.random.fold_in(key_of[11], 71), 0)
    expert_target_keys = jax.random.split(jax.random.fold_in(key_of[2], 1), REQUESTS // REQ_DEV)
    expert_target_turns = jax.random.permutation(jax.random.fold_in(key_of[2], 3), REQUESTS // REQ_DEV)
    expert_target = jax.vmap(lambda own, number: shared_out(jax.random.fold_in(key_of[2], 2), own, number, REQ_DEV, N_SHARD, TOPR, CAP, 2))(expert_target_keys, expert_target_turns).reshape((REQUESTS, TOPR))
    sequence_extent = place_ends(jax.random.randint(key_of[3], (REQUESTS,), 1, HLEN + 1), jax.random.fold_in(key_of[3], 1), 1, HLEN).astype(jnp.int32)
    behaviour_sequence = centred(key_of[4], (REQUESTS, HLEN, DA), 1.0, 6.0, ((0, 256),))
    inner_projection_matrix = centred(key_of[5], (DP, HP), DP ** -0.5, 0.1875)
    student_rating_vector = centred(key_of[6], (HP,), HP ** -0.5, 0.1875)
    asking_matrix = centred(key_of[7], (EXPERTS, DP, DA), DP ** -0.5, 0.1875, ((0, 32),))
    lookup_matrix = centred(key_of[8], (EXPERTS, DA, DA), DA ** -0.5, 0.25, ((0, 32),))
    content_matrix = centred(key_of[9], (EXPERTS, DA, DA), DA ** -0.5, 0.25, ((0, 32),))
    expert_rating_vector = centred(key_of[10], (EXPERTS, DA), 0.2, 1.1953125, ((0, 32),))
    return {"offer_attribute_matrix": offer_attribute_matrix, "kept_offers": kept_offers, "expert_target": expert_target, "sequence_extent": sequence_extent, "behaviour_sequence": behaviour_sequence, "inner_projection_matrix": inner_projection_matrix, "student_rating_vector": student_rating_vector, "asking_matrix": asking_matrix, "lookup_matrix": lookup_matrix, "content_matrix": content_matrix, "expert_rating_vector": expert_rating_vector}


def teacher_one(selected, history_rows, length, expert, asking_matrix, lookup_matrix, content_matrix, expert_rating_vector):
    queries = jnp.dot(selected, asking_matrix[expert], preferred_element_type=jnp.float32).astype(jnp.bfloat16)
    key_rows = jnp.dot(history_rows, lookup_matrix[expert], preferred_element_type=jnp.float32).astype(jnp.bfloat16)
    value_rows = jnp.dot(history_rows, content_matrix[expert], preferred_element_type=jnp.float32).astype(jnp.bfloat16)
    single_attender_span = queries.shape[1] // ATTENDER_GANGS
    query_heads = queries.reshape(KS, ATTENDER_GANGS, single_attender_span).astype(jnp.float32)
    key_heads = key_rows.reshape(HLEN, ATTENDER_GANGS, single_attender_span).astype(jnp.float32)
    value_heads = value_rows.reshape(HLEN, ATTENDER_GANGS, single_attender_span).astype(jnp.float32)
    logits = jnp.einsum('khd,jhd->hkj', query_heads, key_heads) * (single_attender_span ** -0.5)
    visible = jnp.arange(HLEN, dtype=jnp.int32)[None, None, :] < length
    weights = jnp.where(visible, jnp.exp(logits), jnp.float32(0.0))
    attn_probs = (weights / jnp.sum(weights, axis=-1, keepdims=True)).astype(jnp.bfloat16)
    mixed_context = jnp.einsum('hkj,jhd->khd', attn_probs.astype(jnp.float32), value_heads).reshape(KS, ATTENDER_GANGS * single_attender_span)
    return jnp.sum(mixed_context * expert_rating_vector[expert].astype(jnp.float32), axis=-1)


def reference(offer_attribute_matrix, kept_offers, expert_target, sequence_extent, behaviour_sequence, inner_projection_matrix, student_rating_vector, asking_matrix, lookup_matrix, content_matrix, expert_rating_vector):
    offers_in_segment = REQUESTS // N_GROUP
    score_vec = student_rating_vector.astype(jnp.float32)

    def one_block(totals, group_idx):
        grad_w, grad_s = totals
        first_element = group_idx * offers_in_segment
        features = lax.dynamic_slice_in_dim(offer_attribute_matrix, first_element, offers_in_segment, 0)
        chosen_lines = lax.dynamic_slice_in_dim(kept_offers, first_element, offers_in_segment, 0)
        experts = lax.dynamic_slice_in_dim(expert_target, first_element, offers_in_segment, 0)
        lengths = lax.dynamic_slice_in_dim(sequence_extent, first_element, offers_in_segment, 0)
        history_rows = lax.dynamic_slice_in_dim(behaviour_sequence, first_element, offers_in_segment, 0)
        flat_feats = features.reshape(offers_in_segment * CAND, DP)
        preact = jnp.dot(flat_feats, inner_projection_matrix, preferred_element_type=jnp.float32)
        hidden = jnp.maximum(preact, jnp.float32(0.0))
        scores = jnp.sum(hidden * score_vec, axis=-1).reshape(offers_in_segment, CAND)
        exp_scores = jnp.exp(scores)
        student = exp_scores / jnp.sum(exp_scores, axis=-1, keepdims=True)
        selected = jnp.take_along_axis(features, chosen_lines[:, :, None], axis=1)

        def apply_one(item):
            total = jnp.zeros((KS,), jnp.float32)
            for which in range(TOPR):
                total = total + teacher_one(item[0], item[1], item[2], item[3][which], asking_matrix, lookup_matrix, content_matrix, expert_rating_vector)
            return total / TOPR

        mentor_output = lax.map(apply_one, (selected, history_rows, lengths, experts))
        exp_teacher = jnp.exp(mentor_output)
        target = exp_teacher / jnp.sum(exp_teacher, axis=-1, keepdims=True)
        onehot = (chosen_lines[:, :, None] == jnp.arange(CAND, dtype=jnp.int32)[None, None, :]).astype(jnp.float32)
        target_cand = jnp.sum(target[:, :, None] * onehot, axis=1)
        score_grad = (student - target_cand).reshape(offers_in_segment * CAND, 1)
        hidden_grad = (score_grad * score_vec * (preact > 0).astype(jnp.float32)).astype(jnp.bfloat16)
        grad_w = grad_w + lax.dot_general(flat_feats, hidden_grad, (((0,), (0,)), ((), ())), preferred_element_type=jnp.float32)
        grad_s = grad_s + jnp.sum(score_grad * hidden, axis=0)
        return (grad_w, grad_s), None

    start = (jnp.zeros((DP, HP), jnp.float32), jnp.zeros((HP,), jnp.float32))
    (grad_hidden, grad_score), unused = lax.scan(one_block, start, jnp.arange(N_GROUP, dtype=jnp.int32))
    return grad_hidden, grad_score
```

```python
import functools

import jax
import jax.numpy as jnp
from jax import lax
from jax.experimental import pallas as pl
from jax.experimental.pallas import tpu as pltpu
from jax.sharding import Mesh
from jax.sharding import PartitionSpec as P

MESH = pl.DeviceIdType.MESH
F32 = jnp.float32
BF16 = jnp.bfloat16
HEADS = 8
GZ, GX, GY, GC = "group", "shard_0", "shard_1", "shard_2"
SHARD = (GX, GY, GC)
GROUP_SHARD = (GZ, GX, GY, GC)
NX, NY, NZ = 4, 4, 8
SLICE = 96
SPLIT = SLICE * NZ
NT = (((1,), (1,)), ((), ()))
TN = (((0,), (0,)), ((), ()))


def dot(a, b, dims=(((1,), (0,)), ((), ()))):
    return lax.dot_general(a, b, dims, preferred_element_type=F32)


def at(axis, step, size):
    return {axis: lax.rem(lax.axis_index(axis) + (step % size), size)}


def gather_kernel(
    x_ref, kept_ref, w1_ref, v_ref, hist_ref, wq_ref, wk_ref, wv_ref, rat_ref, meta_ref,
    sel_all, hist_all, meta_all, wq_all, wk_all, wr_all, hid_out, st_out, xt_out,
    x_v, w1_v, wv_v, sel_v, wr_v, hid_v, st_v, xt_v, send_sem, recv_sem, load_sem,
):
    z = lax.axis_index(GZ)
    other = {GC: 1 - lax.axis_index(GC)}
    right = {a: at(a, 1, n) for a, n in ((GX, NX), (GY, NY), (GZ, NZ))}
    left = {a: at(a, -1, n) for a, n in ((GX, NX), (GY, NY), (GZ, NZ))}
    used = []

    def send(src, dst, device):
        k = len(used)
        copy = pltpu.make_async_remote_copy(
            src_ref=src, dst_ref=dst, send_sem=send_sem.at[k], recv_sem=recv_sem.at[k],
            device_id=device, device_id_type=MESH,
        )
        copy.start()
        used.append(copy)
        return copy

    local = []

    def load(src, dst):
        copy = pltpu.make_async_copy(src, dst, load_sem.at[len(local)])
        copy.start()
        local.append(copy)
        return copy

    load_x = load(x_ref, x_v)
    load_wv = load(wv_ref, wv_v)
    load_w1 = load(w1_ref, w1_v)

    barrier = pltpu.get_barrier_semaphore()
    peers = [*right.values(), *left.values(), other]
    for peer in peers:
        pl.semaphore_signal(barrier, inc=1, device_id=peer, device_id_type=MESH)
    pl.semaphore_wait(barrier, len(peers))

    def zrows(step, start=0, size=SLICE):
        plane = lax.rem(z + (step % NZ), NZ)
        return pl.ds(pl.multiple_of(plane * SLICE + start, 16), size)

    half = SLICE // 2
    tail = (1024 - SPLIT) // 2
    yR, yL, xR, xL, zR, zL = right[GY], left[GY], right[GX], left[GX], right[GZ], left[GZ]

    zsR = send(wq_ref.at[zrows(0)], wq_all.at[1, zrows(0)], yR)
    zsL = send(wq_ref.at[zrows(0)], wq_all.at[0, zrows(0)], yL)

    def x_hist(h, device, slot):
        return send(hist_ref.at[pl.ds(2 * h, 2)], hist_all.at[slot, 0, pl.ds(2 * h, 2)], device)

    def x_sel(h, device, slot):
        return send(sel_v.at[pl.ds(2 * h, 2)], sel_all.at[slot, 0, pl.ds(2 * h, 2)], device)

    def y_k(h, device, slot):
        rows = pl.ds(256 * h, 256)
        return send(wk_ref.at[rows], wk_all.at[slot, rows], device)

    def y_q(h, device, slot):
        rows = pl.ds(SPLIT + tail * h, tail)
        return send(wq_ref.at[rows], wq_all.at[slot, rows], device)

    histR = {0: x_hist(0, xR, 2)}
    histL = {1: x_hist(1, xL, 1)}
    ykR = {0: y_k(0, yR, 1)}
    ykL = {1: y_k(1, yL, 0)}
    metaR = send(meta_ref, meta_all.at[2, 0], xR)
    metaL = send(meta_ref, meta_all.at[1, 0], xL)
    send(meta_ref, meta_all.at[0, 1], other)
    load(meta_ref, meta_all.at[0, 0])
    load(hist_ref, hist_all.at[0, 0])

    load_x.wait()
    for r in range(4):
        onehot = (
            lax.broadcasted_iota(jnp.int32, (128, 32), 0) == kept_ref[pl.ds(r, 1), :]
        ).astype(F32).astype(BF16)
        sel_v[r] = dot(onehot, x_v[r], TN).astype(BF16)
    selR = {0: x_sel(0, xR, 2)}
    selL = {1: x_sel(1, xL, 1)}
    load(sel_v, sel_all.at[0, 0])

    load_wv.wait()
    head_of = lax.broadcasted_iota(jnp.int32, (16, 512), 1) // 64
    row_of = lax.broadcasted_iota(jnp.int32, (16, 512), 0)
    rating = jnp.where(head_of == row_of, rat_ref[...].astype(F32), 0.0).astype(BF16)
    wr_v[...] = dot(rating, wv_v[...], NT).astype(BF16)
    load(wr_v, wr_all.at[3])

    zsR.wait_recv()
    zsL.wait_recv()
    gA, gB = pl.ds(0, 2), pl.ds(2, 1)

    def z_send(group, step, device, start=0, size=SLICE):
        rows = zrows(step, start, size)
        return send(wq_all.at[group, rows], wq_all.at[group, rows], device)

    aR = [z_send(gA, 0, zR)]
    aL = [z_send(gA, 0, zL)]
    zs2R = send(wq_all.at[1, zrows(0, 0, half)], wq_all.at[2, zrows(0, 0, half)], yR)
    zs2L = send(wq_all.at[0, zrows(0, half, half)], wq_all.at[2, zrows(0, half, half)], yL)
    yqR = {0: y_q(0, yR, 1)}
    yqL = {1: y_q(1, yL, 0)}
    wrR = send(wr_v, wr_all.at[1], yR)
    wrL = send(wr_v, wr_all.at[0], yL)
    histR[1], histL[0] = x_hist(1, xR, 2), x_hist(0, xL, 1)
    selR[1], selL[0] = x_sel(1, xR, 2), x_sel(0, xL, 1)
    ykR[1], ykL[0] = y_k(1, yR, 1), y_k(0, yL, 0)
    yqR[1], yqL[0] = y_q(1, yR, 1), y_q(0, yL, 0)
    send(hist_ref, hist_all.at[0, 1], other)
    send(sel_v, sel_all.at[0, 1], other)

    load_w1.wait()

    @pl.loop(0, 4)
    def _(r):
        rows = pl.ds(pl.multiple_of(r * 128, 128), 128)
        block = x_v[r]
        scores = jnp.zeros((128, 1), F32)
        for q in range(4):
            cols = pl.ds(256 * q, 256)
            hidden = jnp.maximum(dot(block, w1_v[:, cols]), 0.0)
            hid_v[rows, cols] = hidden
            scores = scores + jnp.sum(hidden * v_ref[:, cols], axis=1, keepdims=True)
        weights = jnp.exp(scores)
        st_v[rows, :] = jnp.broadcast_to(weights / jnp.sum(weights, axis=0, keepdims=True), (128, 128))
        xt_v[:, rows] = block.T

    load(hid_v, hid_out)
    load(st_v, st_out)
    load(xt_v, xt_out)

    def x_forward(kind, ref, h, arrived):
        arrived.wait_recv()
        rows = pl.ds(2 * h, 2)
        device, slot = (xR, 2) if h == 0 else (xL, 1)
        piece = ref.at[slot, 0, rows]
        on = send(piece, ref.at[3, 0, rows], device)
        send(piece, ref.at[slot, 1, rows], other)
        return on

    def x_across(ref, slot, h, arrived):
        arrived.wait_recv()
        rows = pl.ds(2 * h, 2)
        send(ref.at[slot, 0, rows], ref.at[slot, 1, rows], other)

    metaR.wait_recv()
    metaL.wait_recv()
    meta2 = send(meta_all.at[2, 0], meta_all.at[3, 0], xR)
    send(meta_all.at[2, 0], meta_all.at[2, 1], other)
    send(meta_all.at[1, 0], meta_all.at[1, 1], other)
    zs2R.wait_recv()
    zs2L.wait_recv()
    bR = [z_send(gB, 0, zR)]
    bL = [z_send(gB, 0, zL)]
    hist2R = x_forward("h", hist_all, 0, histR[0])
    hist2L = x_forward("h", hist_all, 1, histL[1])
    aR[0].wait_recv()
    aR.append(z_send(gA, -1, zR))
    aL[0].wait_recv()
    aL.append(z_send(gA, 1, zL))
    sel2R = x_forward("s", sel_all, 0, selR[0])
    sel2L = x_forward("s", sel_all, 1, selL[1])
    bR[0].wait_recv()
    bR.append(z_send(gB, -1, zR))
    bL[0].wait_recv()
    bL.append(z_send(gB, 1, zL))

    def y_forward(h, ak, aq):
        device, slot = (yR, 1) if h == 0 else (yL, 0)
        ak.wait_recv()
        rows = pl.ds(256 * h, 256)
        k2 = send(wk_all.at[slot, rows], wk_all.at[2, rows], device)
        aq.wait_recv()
        rows = pl.ds(SPLIT + tail * h, tail)
        q2 = send(wq_all.at[slot, rows], wq_all.at[2, rows], device)
        return [k2, q2]

    last = y_forward(0, ykR[0], yqR[0]) + y_forward(1, ykL[1], yqL[1])
    aR[1].wait_recv()
    aR.append(z_send(gA, -2, zR))
    aL[1].wait_recv()
    aL.append(z_send(gA, 2, zL))
    wrR.wait_recv()
    wrL.wait_recv()
    last.append(send(wr_all.at[1], wr_all.at[2], yR))
    bR[1].wait_recv()
    bR.append(z_send(gB, -2, zR))
    bL[1].wait_recv()
    bL.append(z_send(gB, 2, zL))
    meta2.wait_recv()
    send(meta_all.at[3, 0], meta_all.at[3, 1], other)
    x_across(hist_all, 2, 1, histR[1])
    x_across(hist_all, 1, 0, histL[0])
    aR[2].wait_recv()
    aR.append(z_send(gA, -3, zR, 0, half))
    aL[2].wait_recv()
    aL.append(z_send(gA, 3, zL, half, half))
    x_across(sel_all, 2, 1, selR[1])
    x_across(sel_all, 1, 0, selL[0])
    bR[2].wait_recv()
    bR.append(z_send(gB, -3, zR, 0, half))
    bL[2].wait_recv()
    bL.append(z_send(gB, 3, zL, half, half))
    x_across(hist_all, 3, 0, hist2R)
    x_across(hist_all, 3, 1, hist2L)
    x_across(sel_all, 3, 0, sel2R)
    x_across(sel_all, 3, 1, sel2L)

    waited = {
        id(c)
        for c in (
            zsR, zsL, zs2R, zs2L, metaR, metaL, meta2, wrR, wrL, hist2R, hist2L, sel2R, sel2L,
            *histR.values(), *histL.values(), *selR.values(), *selL.values(),
            ykR[0], ykL[1], yqR[0], yqL[1], *aR[:3], *aL[:3], *bR[:3], *bL[:3],
        )
    }
    for copy in used:
        if id(copy) not in waited:
            copy.wait_recv()
    for copy in used:
        copy.wait_send()
    for copy in local:
        if all(copy is not done for done in (load_x, load_wv, load_w1)):
            copy.wait()


def ranker_kernel(
    meta_ref, sel_ref, hist_ref, wq_ref, wk_ref, wq_own, wk_own, wr_ref, out_ref,
    sel_v, hist_v, wq_v, wk_v, wr_v, wide_v, acc_v, list_s, in_sem, w_sem,
):
    x, y, c = lax.axis_index(GX), lax.axis_index(GY), lax.axis_index(GC)
    copies = [
        pltpu.make_async_copy(hist_ref, hist_v, in_sem.at[0]),
        pltpu.make_async_copy(sel_ref, sel_v, in_sem.at[1]),
        pltpu.make_async_copy(wr_ref, wr_v, in_sem.at[2]),
    ]
    weights = []
    for d in range(4):
        if d == 3:
            pair = (wq_own, wk_own)
        else:
            pair = (wq_ref.at[d], wk_ref.at[d])
        weights.append(
            (
                pltpu.make_async_copy(pair[0], wq_v.at[d], w_sem.at[d, 0]),
                pltpu.make_async_copy(pair[1], wk_v.at[d], w_sem.at[d, 1]),
            )
        )
    weights[0][0].start()
    weights[0][1].start()
    for copy in copies:
        copy.start()
    for d in range(1, 4):
        weights[d][0].start()
        weights[d][1].start()
    acc_v[...] = jnp.zeros_like(acc_v)
    for copy in copies:
        copy.wait()

    head_of = lax.broadcasted_iota(jnp.int32, (32, 512), 1) // 64
    slot_row = lax.broadcasted_iota(jnp.int32, (128, 256), 0)

    @pl.loop(0, 4)
    def _(d):
        step = jnp.where(d == 3, 0, jnp.where(d == 2, 2, jnp.where(d == 1, 3, 1)))
        expert = (x * 4 + lax.rem(y + step, 4)) * 2 + c

        def listed(r, count):
            here = lax.shift_right_logical(meta_ref[(r // 4) * 8, lax.rem(r, 4)], expert) & 1
            list_s[count] = r
            return count + here

        count = lax.fori_loop(0, 32, listed, jnp.int32(0))
        for k in range(3):
            list_s[count + k] = 32

        pltpu.make_async_copy(wq_own, wq_v.at[d], w_sem.at[d, 0]).wait()
        pltpu.make_async_copy(wk_own, wk_v.at[d], w_sem.at[d, 1]).wait()
        small = wr_v[d].astype(F32)
        for h in range(HEADS):
            wide_v[pl.ds(32 * h, 32), :] = jnp.broadcast_to(small[h : h + 1, :], (32, 512)).astype(BF16)

        @pl.loop(0, lax.div(count + 3, 4))
        def _(chunk):
            ids = [list_s[chunk * 4 + k] for k in range(4)]
            safe = [jnp.minimum(i, 31) for i in ids]
            rows = jnp.concatenate([sel_v[i] for i in safe], axis=0)
            queries = dot(rows, wq_v[d]).astype(BF16)
            slots = jnp.concatenate([hist_v[i] for i in safe], axis=0)
            keys = dot(slots, wk_v[d]).astype(BF16)
            worth = dot(slots, wide_v[...], NT)
            for k in range(4):
                length = meta_ref[(safe[k] // 4) * 8, 4 + lax.rem(safe[k], 4)]
                mine = queries[32 * k : 32 * k + 32]
                spread = jnp.concatenate(
                    [jnp.where(head_of == h, mine, jnp.zeros_like(mine)) for h in range(HEADS)], axis=0
                )
                logits = dot(keys[128 * k : 128 * k + 128], spread, NT) * 0.125
                w = jnp.where(slot_row < length, jnp.exp(logits), 0.0)
                top = jnp.sum(w * worth[128 * k : 128 * k + 128], axis=0, keepdims=True)
                score = top / jnp.sum(w, axis=0, keepdims=True)
                score = score[:, :128] + score[:, 128:]
                score = score + pltpu.roll(score, 64, 1)
                score = score + pltpu.roll(score, 32, 1)
                acc_v[pl.ds(ids[k], 1), :] += score

    for s in range(8):
        out_ref[s, pl.ds(0, 4), :] = acc_v[pl.ds(4 * s, 4), :]
        out_ref[s, pl.ds(4, 4), :] = jnp.zeros((4, 128), F32)


def reduce_kernel(
    part_ref, kept_ref, v_ref, st_ref, hid_ref, xt_ref,
    gh_ref, gs_ref,
    hid_v, xt_v, hg_v, t_v, ga_s, ga_r, own_v, b1_s, b1_r, b2_s, b2_r, a1_v, a2_v,
    c1_s, c1_r, c2_s, c2_r, fin_v, d_s, d_r, e_v, s0_v, sx_v, sy_v, sz_v, send_sem, recv_sem, load_sem,
):
    x, y, z, c = (lax.axis_index(a) for a in (GX, GY, GZ, GC))
    other = {GC: 1 - c}
    used = []

    def send(src, dst, device):
        k = len(used)
        copy = pltpu.make_async_remote_copy(
            src_ref=src, dst_ref=dst, send_sem=send_sem.at[k], recv_sem=recv_sem.at[k],
            device_id=device, device_id_type=MESH,
        )
        copy.start()
        used.append(copy)
        return copy

    load_h = pltpu.make_async_copy(hid_ref, hid_v.at[pl.ds(0, 512)], load_sem.at[0])
    load_h.start()
    load_x = pltpu.make_async_copy(xt_ref, xt_v, load_sem.at[1])
    load_x.start()

    xs = [at(GX, k, NX) for k in (1, 2, 3)]
    ys = [at(GY, k, NY) for k in (1, 2, 3)]
    zs = [at(GZ, k, NZ) for k in range(1, NZ)]
    diag = [{**d, **other} for d in xs]
    peers = [*xs, *ys, *zs, *diag, other]
    barrier = pltpu.get_barrier_semaphore()
    for peer in peers:
        pl.semaphore_signal(barrier, inc=1, device_id=peer, device_id_type=MESH)
    pl.semaphore_wait(barrier, len(peers))

    back = []
    slot_of = {1: 1, 2: 3, 3: 2}
    for k in (1, 2, 3):
        s = slot_of[k]
        back.append(send(part_ref.at[2 * s], t_v.at[2 * s], xs[k - 1]))
        back.append(send(part_ref.at[2 * s + 1], t_v.at[2 * s + 1], diag[k - 1]))
    back.append(send(part_ref.at[1], t_v.at[1], other))
    t_v[0] = part_ref[0]
    load_h.wait()
    load_x.wait()
    for copy in back:
        copy.wait_recv()
    teacher = t_v[0]
    for k in range(1, 8):
        teacher = teacher + t_v[k]
    live = lax.broadcasted_iota(jnp.int32, (8, 128), 1) < 32
    risen = jnp.where(live, jnp.exp(teacher / 6.0), 0.0)
    t_v[0] = risen / jnp.sum(risen, axis=1, keepdims=True)

    for r in range(4):
        rows = pl.ds(128 * r, 128)
        spots = lax.broadcasted_iota(jnp.int32, (128, 32), 0) == kept_ref[pl.ds(r, 1), :]
        aim = jnp.sum(jnp.where(spots, t_v[0, pl.ds(r, 1), pl.ds(0, 32)], 0.0), axis=1, keepdims=True)
        grad = st_ref[rows, pl.ds(0, 1)] - aim
        for q in range(4):
            cols = pl.ds(256 * q, 256)
            hidden = hid_v[rows, cols]
            hg_v[rows, cols] = jnp.where(hidden > 0.0, grad * v_ref[:, cols], 0.0).astype(BF16)
            hid_v[pl.ds(512 + 8 * r, 8), cols] = jnp.sum((grad * hidden).reshape(16, 8, 256), axis=0)
    total = hid_v[pl.ds(512, 8), :] + hid_v[pl.ds(520, 8), :] + hid_v[pl.ds(528, 8), :] + hid_v[pl.ds(536, 8), :]
    row = jnp.sum(total, axis=0, keepdims=True)
    for k in range(8):
        s0_v[0, pl.ds(k, 1), :] = row[:, 128 * k : 128 * k + 128]
    sa = send(s0_v.at[0], s0_v.at[1], other)

    core = []

    def rows_of(k, side):
        return xt_v[pl.ds(4 * k, 4), side].reshape(128, 512)

    for k in range(4):
        ga_s[pl.ds(4 * k, 4)] = dot(rows_of(k, 1 - c), hg_v[...]).astype(BF16).reshape(4, 32, 1024)
        core.append(send(ga_s.at[pl.ds(4 * k, 4)], ga_r.at[pl.ds(4 * k, 4)], other))
    for k in range(4):
        own_v[pl.ds(4 * k, 4)] = dot(rows_of(k, c), hg_v[...]).reshape(4, 32, 1024)
    for k in range(4):
        core[k].wait_recv()
        blocks = pl.ds(4 * k, 4)
        own_v[blocks] = own_v[blocks] + ga_r[blocks].astype(F32)
    sa.wait_recv()
    sx_v[x] = s0_v[0] + s0_v[1]

    n1, n2 = pl.ds(0, 512), pl.ds(512, 512)
    first, second, sb = [], [], []
    for k in (2, 1, 3):
        tx, ty = xs[k - 1][GX], ys[k - 1][GY]
        b1_s[k - 1] = own_v[pl.ds(4 * tx, 4), :, n1].astype(BF16)
        first.append(send(b1_s.at[k - 1], b1_r.at[k - 1], xs[k - 1]))
        for j in range(4):
            b2_s[k - 1, j] = own_v[4 * j + ty, :, n2].astype(BF16)
        second.append(send(b2_s.at[k - 1], b2_r.at[k - 1], ys[k - 1]))
        sb.append(send(sx_v.at[x], sx_v.at[x], xs[k - 1]))
    for copy in sb:
        copy.wait_recv()
    sy_v[y] = (sx_v[0] + sx_v[1]) + (sx_v[2] + sx_v[3])
    sc = [send(sy_v.at[y], sy_v.at[y], ys[k]) for k in range(3)]
    for copy in first:
        copy.wait_recv()
    a1_v[...] = own_v[pl.ds(4 * x, 4), :, n1] + (
        b1_r[0].astype(F32) + b1_r[1].astype(F32) + b1_r[2].astype(F32)
    )
    third = []
    for k in (2, 1, 3):
        c1_s[k - 1] = a1_v[ys[k - 1][GY]].astype(BF16)
        third.append(send(c1_s.at[k - 1], c1_r.at[k - 1], ys[k - 1]))
    for copy in second:
        copy.wait_recv()
    for j in range(4):
        a2_v[j] = own_v[4 * j + y, :, n2] + (
            b2_r[0, j].astype(F32) + b2_r[1, j].astype(F32) + b2_r[2, j].astype(F32)
        )
    for k in (2, 1, 3):
        c2_s[k - 1] = a2_v[xs[k - 1][GX]].astype(BF16)
        third.append(send(c2_s.at[k - 1], c2_r.at[k - 1], xs[k - 1]))
    for copy in sc:
        copy.wait_recv()
    sz_v[z] = (sy_v[0] + sy_v[1]) + (sy_v[2] + sy_v[3])
    sd = [send(sz_v.at[z], sz_v.at[z], zs[k]) for k in range(NZ - 1)]
    for copy in third:
        copy.wait_recv()
    fin1 = a1_v[y] + (c1_r[0].astype(F32) + c1_r[1].astype(F32) + c1_r[2].astype(F32))
    fin2 = a2_v[x] + (c2_r[0].astype(F32) + c2_r[1].astype(F32) + c2_r[2].astype(F32))
    for k in range(4):
        fin_v[k] = fin1[:, 128 * k : 128 * k + 128]
        fin_v[4 + k] = fin2[:, 128 * k : 128 * k + 128]
    d_s[...] = fin_v[...].astype(BF16)

    fourth = []
    for k in (4, 3, 5, 2, 6, 1, 7):
        fourth.append(send(d_s.at[zs[k - 1][GZ]], d_r.at[k - 1], zs[k - 1]))
    for copy in fourth:
        copy.wait_recv()
    whole = fin_v[z]
    for k in range(NZ - 1):
        whole = whole + d_r[k].astype(F32)
    e_v[z] = whole
    fifth = [send(e_v.at[z], e_v.at[z], zs[k - 1]) for k in (4, 3, 5, 2, 6, 1, 7)]
    for copy in sd:
        copy.wait_recv()
    gs = sz_v[0]
    for k in range(1, NZ):
        gs = gs + sz_v[k]
    gs_ref[...] = gs
    for copy in fifth:
        copy.wait_recv()
    for k in range(NZ):
        gh_ref[:, pl.ds(128 * k, 128)] = e_v[k]
    for copy in used:
        copy.wait_send()


def any_specs(n):
    return [pl.BlockSpec(memory_space=pl.ANY)] * n


def vmem_specs(n):
    return [pl.BlockSpec(memory_space=pltpu.VMEM)] * n


def shapes(*items):
    return [jax.ShapeDtypeStruct(s, t) for s, t in items]


def body(
    offer_attribute_matrix,
    kept_offers,
    expert_target,
    sequence_extent,
    behaviour_sequence,
    inner_projection_matrix,
    student_rating_vector,
    asking_matrix,
    lookup_matrix,
    content_matrix,
    expert_rating_vector,
):
    bits = jnp.sum(jnp.left_shift(jnp.int32(1), expert_target), axis=1)
    info = jnp.concatenate([bits, sequence_extent])
    meta = jnp.zeros((8, 128), jnp.int32).at[0, :8].set(info)
    v_row = student_rating_vector.astype(F32).reshape(1, 1024)
    wq, wk, wv = asking_matrix[0], lookup_matrix[0], content_matrix[0]

    sel_all, hist_all, meta_all, wq_all, wk_all, wr_all, hidden, student, turned = pl.pallas_call(
        gather_kernel,
        out_shape=shapes(
            ((4, 2, 4, 32, 1024), BF16),
            ((4, 2, 4, 128, 512), BF16),
            ((4, 2, 8, 128), jnp.int32),
            ((3, 1024, 512), BF16),
            ((3, 512, 512), BF16),
            ((4, 16, 512), BF16),
            ((512, 1024), F32),
            ((512, 128), F32),
            ((1024, 512), BF16),
        ),
        in_specs=[
            *any_specs(1), *vmem_specs(1), *any_specs(1), *vmem_specs(1), *any_specs(4), *vmem_specs(1),
            *any_specs(1),
        ],
        out_specs=any_specs(9),
        scratch_shapes=[
            pltpu.VMEM((4, 128, 1024), BF16),
            pltpu.VMEM((1024, 1024), BF16),
            pltpu.VMEM((512, 512), BF16),
            pltpu.VMEM((4, 32, 1024), BF16),
            pltpu.VMEM((16, 512), BF16),
            pltpu.VMEM((512, 1024), F32),
            pltpu.VMEM((512, 128), F32),
            pltpu.VMEM((1024, 512), BF16),
            pltpu.SemaphoreType.DMA((80,)),
            pltpu.SemaphoreType.DMA((80,)),
            pltpu.SemaphoreType.DMA((12,)),
        ],
        compiler_params=pltpu.CompilerParams(
            collective_id=0, has_side_effects=True, vmem_limit_bytes=40 * 2**20
        ),
        name="gather_requests_and_experts",
    )(
        offer_attribute_matrix, kept_offers, inner_projection_matrix, v_row, behaviour_sequence,
        wq, wk, wv, expert_rating_vector, meta,
    )

    part = pl.pallas_call(
        ranker_kernel,
        out_shape=jax.ShapeDtypeStruct((8, 8, 128), F32),
        in_specs=[pl.BlockSpec(memory_space=pltpu.SMEM), *any_specs(7)],
        out_specs=pl.BlockSpec(memory_space=pltpu.VMEM),
        scratch_shapes=[
            pltpu.VMEM((32, 32, 1024), BF16),
            pltpu.VMEM((32, 128, 512), BF16),
            pltpu.VMEM((4, 1024, 512), BF16),
            pltpu.VMEM((4, 512, 512), BF16),
            pltpu.VMEM((4, 16, 512), BF16),
            pltpu.VMEM((256, 512), BF16),
            pltpu.VMEM((40, 128), F32),
            pltpu.SMEM((40,), jnp.int32),
            pltpu.SemaphoreType.DMA((3,)),
            pltpu.SemaphoreType.DMA((4, 2)),
        ],
        compiler_params=pltpu.CompilerParams(vmem_limit_bytes=48 * 2**20),
        name="rankers",
    )(
        meta_all.reshape(64, 128), sel_all.reshape(32, 32, 1024), hist_all.reshape(32, 128, 512),
        wq_all, wk_all, wq, wk, wr_all,
    )

    grad_hidden, grad_score = pl.pallas_call(
        reduce_kernel,
        out_shape=shapes(((32, 1024), F32), ((8, 128), F32)),
        in_specs=[*vmem_specs(4), *any_specs(2)],
        out_specs=vmem_specs(2),
        scratch_shapes=[
            pltpu.VMEM((544, 1024), F32),
            pltpu.VMEM((16, 2, 32, 512), BF16),
            pltpu.VMEM((512, 1024), BF16),
            pltpu.VMEM((8, 8, 128), F32),
            pltpu.VMEM((16, 32, 1024), BF16),
            pltpu.VMEM((16, 32, 1024), BF16),
            pltpu.VMEM((16, 32, 1024), F32),
            *[pltpu.VMEM((3, 4, 32, 512), BF16) for _ in range(4)],
            *[pltpu.VMEM((4, 32, 512), F32) for _ in range(2)],
            *[pltpu.VMEM((3, 32, 512), BF16) for _ in range(4)],
            pltpu.VMEM((8, 32, 128), F32),
            pltpu.VMEM((8, 32, 128), BF16),
            pltpu.VMEM((7, 32, 128), BF16),
            pltpu.VMEM((8, 32, 128), F32),
            pltpu.VMEM((2, 8, 128), F32),
            pltpu.VMEM((4, 8, 128), F32),
            pltpu.VMEM((4, 8, 128), F32),
            pltpu.VMEM((8, 8, 128), F32),
            pltpu.SemaphoreType.DMA((64,)),
            pltpu.SemaphoreType.DMA((64,)),
            pltpu.SemaphoreType.DMA((2,)),
        ],
        compiler_params=pltpu.CompilerParams(
            collective_id=1, has_side_effects=True, vmem_limit_bytes=40 * 2**20
        ),
        name="targets_and_gradients",
    )(part, kept_offers, v_row, student, hidden, turned.reshape(16, 2, 32, 512))
    return grad_hidden, grad_score.reshape(1024)


def solution(mesh):
    torus = Mesh(mesh.devices.reshape(mesh.shape["group"], NX, NY, 2), GROUP_SHARD)
    return jax.shard_map(
        body,
        mesh=torus,
        in_specs=(
            P(GROUP_SHARD, None, None),
            P(GROUP_SHARD, None),
            P(GROUP_SHARD, None),
            P(GROUP_SHARD),
            P(GROUP_SHARD, None, None),
            P(),
            P(),
            P(SHARD, None, None),
            P(SHARD, None, None),
            P(SHARD, None, None),
            P(SHARD, None),
        ),
        out_specs=(P(SHARD, None), P()),
        check_vma=False,
    )
```

```python
import functools

import jax
import jax.numpy as jnp
from jax import lax
from jax.experimental import pallas as pl
from jax.experimental.pallas import tpu as pltpu
from jax.sharding import Mesh
from jax.sharding import PartitionSpec as P

MESH = pl.DeviceIdType.MESH
F32 = jnp.float32
BF16 = jnp.bfloat16
HEADS = 8
GZ, GX, GY, GC = "group", "shard_0", "shard_1", "shard_2"
SHARD = (GX, GY, GC)
GROUP_SHARD = (GZ, GX, GY, GC)
NX, NY, NZ = 4, 4, 8
SLICE = 96
SPLIT = SLICE * NZ
NT = (((1,), (1,)), ((), ()))
TN = (((0,), (0,)), ((), ()))


def dot(a, b, dims=(((1,), (0,)), ((), ()))):
    return lax.dot_general(a, b, dims, preferred_element_type=F32)


class Sent:
    def __init__(self, copy):
        self.copy, self.arrived = copy, False
        copy.start()

    def wait_recv(self):
        if not self.arrived:
            self.copy.wait_recv()
        self.arrived = True

    def wait_send(self):
        self.copy.wait_send()


def at(axis, step, size):
    return {axis: lax.rem(lax.axis_index(axis) + (step % size), size)}


def whole_kernel(
    x_ref, kept_in, target_in, extent_in, w1_ref, v_in, hist_ref, wq_ref, wk_ref, wv_ref, rat_in,
    gh_ref, gs_ref,
    sel0, sel1, sel2, sel3, hist0, hist1, hist2, hist3,
    meta_all, meta_s, wq_all, wk_all, wr_all, wide_v, acc_v,
    kept_ref, target_ref, extent_ref, v_ref, rat_ref,
    x_v, w1_v, wv_v, hid_v, st_v, xt_v, sum_v,
    hg_v, t_v, ga_s, ga_r, own_v, b1_s, b1_r, b2_s, b2_r, a1_v, a2_v,
    c1_s, c1_r, c2_s, c2_r, fin_v, d_s, d_r, e_v, s0_v, sx_v, sy_v, sz_v, send_sem, recv_sem, load_sem,
):
    sel_p, hist_p = (sel0, sel1, sel2, sel3), (hist0, hist1, hist2, hist3)
    x, y, z, c = (lax.axis_index(a) for a in (GX, GY, GZ, GC))
    other = {GC: 1 - c}
    used = []

    def send(src, dst, device):
        k = len(used)
        used.append(
            Sent(
                pltpu.make_async_remote_copy(
                    src_ref=src, dst_ref=dst, send_sem=send_sem.at[k], recv_sem=recv_sem.at[k],
                    device_id=device, device_id_type=MESH,
                )
            )
        )
        return used[-1]

    loads = []

    def load(src, dst):
        copy = pltpu.make_async_copy(src, dst, load_sem.at[len(loads)])
        copy.start()
        loads.append(copy)
        return copy

    load_small = [
        load(src, dst)
        for src, dst in (
            (target_in, target_ref), (extent_in, extent_ref), (kept_in, kept_ref), (rat_in, rat_ref),
            (v_in, v_ref),
        )
    ]
    load_x = load(x_ref, x_v)
    load_wv = load(wv_ref, wv_v)
    load_own = [load(hist_ref, hist0.at[0]), load(wq_ref, wq_all.at[0]), load(wk_ref, wk_all.at[0])]
    load_w1 = load(w1_ref, w1_v)

    xs = [at(GX, k, NX) for k in (1, 2, 3)]
    ys = [at(GY, k, NY) for k in (1, 2, 3)]
    zs = [at(GZ, k, NZ) for k in range(1, NZ)]
    diag = [{**d, **other} for d in xs]
    peers = [*xs, *ys, *zs, *diag, other]
    barrier = pltpu.get_barrier_semaphore()
    for peer in peers:
        pl.semaphore_signal(barrier, inc=1, device_id=peer, device_id_type=MESH)
    pl.semaphore_wait(barrier, len(peers))

    def zrows(step, start=0, size=SLICE):
        plane = lax.rem(z + (step % NZ), NZ)
        return pl.ds(pl.multiple_of(plane * SLICE + start, 16), size)

    half = SLICE // 2
    tail = (1024 - SPLIT) // 2
    xR, xL, yR, yL, zR, zL = xs[0], xs[2], ys[0], ys[2], zs[0], zs[6]

    zsR = send(wq_ref.at[zrows(0)], wq_all.at[2, zrows(0)], yR)
    zsL = send(wq_ref.at[zrows(0)], wq_all.at[1, zrows(0)], yL)

    def two(h):
        return pl.ds(2 * h, 2)

    def x_hist(h, device, slot):
        return send(hist_ref.at[two(h)], hist_p[slot].at[0, two(h)], device)

    def x_sel(h, device, slot):
        return send(sel0.at[0, two(h)], sel_p[slot].at[0, two(h)], device)

    def y_k(h, device, slot):
        rows = pl.ds(256 * h, 256)
        return send(wk_ref.at[rows], wk_all.at[slot, rows], device)

    def y_q(h, device, slot):
        rows = pl.ds(SPLIT + tail * h, tail)
        return send(wq_ref.at[rows], wq_all.at[slot, rows], device)

    histR, histL = {0: x_hist(0, xR, 2)}, {1: x_hist(1, xL, 1)}
    ykR, ykL = {0: y_k(0, yR, 2)}, {1: y_k(1, yL, 1)}
    for copy in load_small:
        copy.wait()
    bits = jnp.sum(jnp.left_shift(jnp.int32(1), target_ref[...]), axis=1, keepdims=True)
    meta_all[0, 0] = jnp.zeros((8, 128), jnp.int32)
    meta_all[0, 0, pl.ds(0, 4), :] = jnp.broadcast_to(bits, (4, 128))
    meta_all[0, 0, pl.ds(4, 1), pl.ds(0, 4)] = extent_ref[...]
    metaR = send(meta_all.at[0, 0], meta_all.at[2, 0], xR)
    metaL = send(meta_all.at[0, 0], meta_all.at[1, 0], xL)
    meta_on = [send(meta_all.at[0, 0], meta_all.at[0, 1], other)]

    load_x.wait()
    for r in range(4):
        onehot = (
            lax.broadcasted_iota(jnp.int32, (128, 32), 0) == kept_ref[pl.ds(r, 1), :]
        ).astype(F32).astype(BF16)
        sel0[0, r] = dot(onehot, x_v[r], TN).astype(BF16)
    selR, selL = {0: x_sel(0, xR, 2)}, {1: x_sel(1, xL, 1)}

    load_wv.wait()
    head_wide = lax.broadcasted_iota(jnp.int32, (16, 512), 1) // 64
    row_of = lax.broadcasted_iota(jnp.int32, (16, 512), 0)
    rating = jnp.where(head_wide == row_of, rat_ref[...].astype(F32), 0.0).astype(BF16)
    wr_all[0] = dot(rating, wv_v[...], NT).astype(BF16)
    wrR = send(wr_all.at[0], wr_all.at[2], yR)
    wrL = send(wr_all.at[0], wr_all.at[1], yL)

    zsR.wait_recv()
    zsL.wait_recv()
    gA, gB = pl.ds(1, 2), pl.ds(3, 1)

    def z_send(group, step, device, start=0, size=SLICE):
        rows = zrows(step, start, size)
        return send(wq_all.at[group, rows], wq_all.at[group, rows], device)

    aR, aL = [z_send(gA, 0, zR)], [z_send(gA, 0, zL)]
    zs2R = send(wq_all.at[2, zrows(0, 0, half)], wq_all.at[3, zrows(0, 0, half)], yR)
    zs2L = send(wq_all.at[1, zrows(0, half, half)], wq_all.at[3, zrows(0, half, half)], yL)
    yqR, yqL = {0: y_q(0, yR, 2)}, {1: y_q(1, yL, 1)}
    histR[1], histL[0] = x_hist(1, xR, 2), x_hist(0, xL, 1)
    selR[1], selL[0] = x_sel(1, xR, 2), x_sel(0, xL, 1)
    ykR[1], ykL[0] = y_k(1, yR, 2), y_k(0, yL, 1)
    yqR[1], yqL[0] = y_q(1, yR, 2), y_q(0, yL, 1)
    on = {0: [send(hist_ref, hist0.at[1], other), send(sel0.at[0], sel0.at[1], other)], 1: [], 2: [], 3: []}

    def tower(r):
        rows = pl.ds(128 * r, 128)
        block = x_v[r]
        scores = jnp.zeros((128, 1), F32)
        for q in range(4):
            cols = pl.ds(256 * q, 256)
            hidden = jnp.maximum(dot(block, w1_v[:, cols]), 0.0)
            hid_v[rows, cols] = hidden
            scores = scores + jnp.sum(hidden * v_ref[:, cols].astype(F32), axis=1, keepdims=True)
        weights = jnp.exp(scores)
        st_v[rows, :] = jnp.broadcast_to(weights / jnp.sum(weights, axis=0, keepdims=True), (128, 128))
        xt_v[:, rows] = block.T

    load_w1.wait()
    tower(0)

    def x_across(refs, slot, h, arrived):
        arrived.wait_recv()
        on[slot].append(send(refs[slot].at[0, two(h)], refs[slot].at[1, two(h)], other))

    def x_forward(refs, h, arrived):
        arrived.wait_recv()
        device, slot = (xR, 2) if h == 0 else (xL, 1)
        sent = send(refs[slot].at[0, two(h)], refs[3].at[0, two(h)], device)
        x_across(refs, slot, h, arrived)
        return sent

    def y_forward(h, ak, aq):
        device, slot = (yR, 2) if h == 0 else (yL, 1)
        ak.wait_recv()
        rows = pl.ds(256 * h, 256)
        send(wk_all.at[slot, rows], wk_all.at[3, rows], device)
        aq.wait_recv()
        rows = pl.ds(SPLIT + tail * h, tail)
        send(wq_all.at[slot, rows], wq_all.at[3, rows], device)

    metaR.wait_recv()
    metaL.wait_recv()
    meta2 = send(meta_all.at[2, 0], meta_all.at[3, 0], xR)
    meta_on.append(send(meta_all.at[2, 0], meta_all.at[2, 1], other))
    meta_on.append(send(meta_all.at[1, 0], meta_all.at[1, 1], other))
    zs2R.wait_recv()
    zs2L.wait_recv()
    bR, bL = [z_send(gB, 0, zR)], [z_send(gB, 0, zL)]
    tower(1)
    hist2R = x_forward(hist_p, 0, histR[0])
    hist2L = x_forward(hist_p, 1, histL[1])
    aR[0].wait_recv()
    aR.append(z_send(gA, -1, zR))
    aL[0].wait_recv()
    aL.append(z_send(gA, 1, zL))
    tower(2)
    sel2R = x_forward(sel_p, 0, selR[0])
    sel2L = x_forward(sel_p, 1, selL[1])
    wrR.wait_recv()
    wrL.wait_recv()
    wr2 = send(wr_all.at[2], wr_all.at[3], yR)
    meta2.wait_recv()
    meta_on.append(send(meta_all.at[3, 0], meta_all.at[3, 1], other))
    bR[0].wait_recv()
    bR.append(z_send(gB, -1, zR))
    bL[0].wait_recv()
    bL.append(z_send(gB, 1, zL))
    tower(3)
    y_forward(0, ykR[0], yqR[0])
    y_forward(1, ykL[1], yqL[1])
    aR[1].wait_recv()
    aR.append(z_send(gA, -2, zR))
    aL[1].wait_recv()
    aL.append(z_send(gA, 2, zL))
    bR[1].wait_recv()
    bR.append(z_send(gB, -2, zR))
    bL[1].wait_recv()
    bL.append(z_send(gB, 2, zL))
    for copy in meta_on:
        copy.wait_recv()
    info = [
        load(meta_all.at[k // 2, k % 2], meta_s.at[pl.ds(8 * k, 8)]) for k in range(8)
    ]
    acc_v[...] = jnp.zeros_like(acc_v)

    head_of = lax.broadcasted_iota(jnp.int32, (32, 512), 1) // 64
    slot_row = lax.broadcasted_iota(jnp.int32, (128, 256), 0)
    out_row = lax.broadcasted_iota(jnp.int32, (8, 128), 0)

    def ranked(d, p):
        step = jnp.where(d == 3, 2, jnp.where(d == 2, 3, jnp.where(d == 1, 1, 0)))
        expert = (x * 4 + lax.rem(y + step, 4)) * 2 + c
        places = []
        for core in range(2):
            base = 16 * p + 8 * core
            seen = jnp.int32(0)
            ids, found = [jnp.int32(0)] * 2, [jnp.int32(0)] * 2
            for i in range(4):
                here = lax.shift_right_logical(meta_s[base + i, 0], expert) & 1
                for j in range(2):
                    hit = jnp.where(seen == j, here, 0)
                    ids[j] = ids[j] + i * hit
                    found[j] = found[j] + hit
                seen = seen + here
            places += [(core, ids[j], found[j]) for j in range(2)]
        rows = jnp.concatenate([sel_p[p][core, i] for core, i, _ in places], axis=0)
        queries = dot(rows, wq_all[d]).astype(BF16)
        slots = jnp.concatenate([hist_p[p][core, i] for core, i, _ in places], axis=0)
        keys = dot(slots, wk_all[d]).astype(BF16)
        worth = dot(slots, wide_v[d])
        for k, (core, i, found) in enumerate(places):
            length = meta_s[16 * p + 8 * core + 4, i]
            mine = queries[32 * k : 32 * k + 32]
            spread = jnp.concatenate(
                [jnp.where(head_of == h, mine, jnp.zeros_like(mine)) for h in range(HEADS)], axis=0
            )
            logits = dot(keys[128 * k : 128 * k + 128], spread, NT) * 0.125
            w = jnp.where(slot_row < length, jnp.exp(logits), 0.0)
            top = jnp.sum(w * worth[128 * k : 128 * k + 128], axis=0, keepdims=True)
            score = top / jnp.sum(w, axis=0, keepdims=True)
            score = score[:, :128] + score[:, 128:]
            score = score + pltpu.roll(score, 64, 1)
            score = score + pltpu.roll(score, 32, 1)
            mark = out_row == jnp.where(found == 1, i, -1)
            acc_v[p, core] = acc_v[p, core] + jnp.where(mark, score, 0.0)

    x_across(hist_p, 2, 1, histR[1])
    x_across(hist_p, 1, 0, histL[0])
    x_across(sel_p, 2, 1, selR[1])
    x_across(sel_p, 1, 0, selL[0])
    aR[2].wait_recv()
    aR.append(z_send(gA, -3, zR, 0, half))
    aL[2].wait_recv()
    aL.append(z_send(gA, 3, zL, half, half))
    wr2.wait_recv()

    @pl.loop(0, 4)
    def _(d):
        small = wr_all[d].astype(F32)
        wide = [jnp.broadcast_to(small[h : h + 1, :], (32, 512)) for h in range(HEADS)]
        wide_v[d] = jnp.concatenate(wide, axis=0).T.astype(BF16)

    for copy in (*info, *load_own):
        copy.wait()
    for copy in (*on[0], *on[1], *on[2]):
        copy.wait_recv()
    for p in range(3):
        ranked(0, p)
    bR[2].wait_recv()
    bR.append(z_send(gB, -3, zR, 0, half))
    bL[2].wait_recv()
    bL.append(z_send(gB, 3, zL, half, half))
    for copy in (*ykR.values(), *ykL.values(), *yqR.values(), *yqL.values(), *aR, *aL):
        copy.wait_recv()

    @pl.loop(1, 3)
    def _(d):
        for p in range(3):
            ranked(d, p)

    x_across(hist_p, 3, 0, hist2R)
    x_across(hist_p, 3, 1, hist2L)
    x_across(sel_p, 3, 0, sel2R)
    x_across(sel_p, 3, 1, sel2L)
    for copy in used:
        copy.wait_recv()
    for p in range(3):
        ranked(3, p)

    @pl.loop(0, 4)
    def _(d):
        ranked(d, 3)

    back = []
    slot_of = {1: 1, 2: 3, 3: 2}
    for k in (1, 2, 3):
        s = slot_of[k]
        back.append(send(acc_v.at[s, 0], t_v.at[2 * s], xs[k - 1]))
        back.append(send(acc_v.at[s, 1], t_v.at[2 * s + 1], diag[k - 1]))
    back.append(send(acc_v.at[0, 1], t_v.at[1], other))
    t_v[0] = acc_v[0, 0]
    for copy in back:
        copy.wait_recv()
    teacher = t_v[0]
    for k in range(1, 8):
        teacher = teacher + t_v[k]
    live = lax.broadcasted_iota(jnp.int32, (8, 128), 1) < 32
    risen = jnp.where(live, jnp.exp(teacher / 6.0), 0.0)
    t_v[0] = risen / jnp.sum(risen, axis=1, keepdims=True)

    for r in range(4):
        rows = pl.ds(128 * r, 128)
        spots = lax.broadcasted_iota(jnp.int32, (128, 32), 0) == kept_ref[pl.ds(r, 1), :]
        aim = jnp.sum(jnp.where(spots, t_v[0, pl.ds(r, 1), pl.ds(0, 32)], 0.0), axis=1, keepdims=True)
        grad = st_v[rows, pl.ds(0, 1)] - aim
        for q in range(4):
            cols = pl.ds(256 * q, 256)
            hidden = hid_v[rows, cols]
            hg_v[rows, cols] = jnp.where(hidden > 0.0, grad * v_ref[:, cols].astype(F32), 0.0).astype(BF16)
            sum_v[pl.ds(8 * r, 8), cols] = jnp.sum((grad * hidden).reshape(16, 8, 256), axis=0)
    row = jnp.sum(sum_v[...], axis=0, keepdims=True)
    for k in range(8):
        s0_v[0, pl.ds(k, 1), :] = row[:, 128 * k : 128 * k + 128]
    sa = send(s0_v.at[0], s0_v.at[1], other)

    core = []

    def rows_of(k, side):
        return jnp.concatenate(
            [xt_v[pl.ds(pl.multiple_of(64 * (4 * k + j) + 32 * side, 32), 32), :] for j in range(4)], axis=0
        )

    for k in range(4):
        ga_s[pl.ds(4 * k, 4)] = dot(rows_of(k, 1 - c), hg_v[...]).astype(BF16).reshape(4, 32, 1024)
        core.append(send(ga_s.at[pl.ds(4 * k, 4)], ga_r.at[pl.ds(4 * k, 4)], other))
    for k in range(4):
        own_v[pl.ds(4 * k, 4)] = dot(rows_of(k, c), hg_v[...]).reshape(4, 32, 1024)
    for k in range(4):
        core[k].wait_recv()
        blocks = pl.ds(4 * k, 4)
        own_v[blocks] = own_v[blocks] + ga_r[blocks].astype(F32)
    sa.wait_recv()
    sx_v[x] = s0_v[0] + s0_v[1]

    n1, n2 = pl.ds(0, 512), pl.ds(512, 512)

    def along_x(side, h):
        return own_v[pl.ds(4 * side[GX] + 2 * h, 2), :, n1]

    def along_y(side, h):
        return jnp.stack([own_v[4 * (2 * h + j) + side[GY], :, n2] for j in range(2)])

    ways = ((along_x, xs, b1_s, b1_r), (along_y, ys, b2_s, b2_r))
    relay, direct = [], []
    for part, sides, out, into in ways:
        for h, device in ((0, sides[0]), (1, sides[2])):
            out[0, pl.ds(2 * h, 2)] = part(sides[1], h).astype(BF16)
            relay.append(send(out.at[0, pl.ds(2 * h, 2)], into.at[0, pl.ds(2 * h, 2)], device))
    sb = [send(sx_v.at[x], sx_v.at[x], xs[k]) for k in range(3)]
    for part, sides, out, into in ways:
        for h, device in ((1, sides[0]), (0, sides[2])):
            k = 2 - h
            out[k, pl.ds(2 * h, 2)] = part(device, h).astype(BF16)
            direct.append(send(out.at[k, pl.ds(2 * h, 2)], into.at[k, pl.ds(2 * h, 2)], device))
    for n, (part, sides, out, into) in enumerate(ways):
        for h, device in ((0, sides[0]), (1, sides[2])):
            relay[2 * n + h].wait_recv()
            k = 1 + h
            rows = pl.ds(2 * h, 2)
            out[k, rows] = (part(device, h) + into[0, rows].astype(F32)).astype(BF16)
            direct.append(send(out.at[k, rows], into.at[k, rows], device))
    for copy in sb:
        copy.wait_recv()
    sy_v[y] = (sx_v[0] + sx_v[1]) + (sx_v[2] + sx_v[3])
    sc = [send(sy_v.at[y], sy_v.at[y], ys[k]) for k in range(3)]
    for copy in direct:
        copy.wait_recv()
    a1_v[...] = own_v[pl.ds(4 * x, 4), :, n1] + (b1_r[1].astype(F32) + b1_r[2].astype(F32))
    for j in range(4):
        a2_v[j] = own_v[4 * j + y, :, n2] + (b2_r[1, j].astype(F32) + b2_r[2, j].astype(F32))
    third = []
    for k in (2, 1, 3):
        c1_s[k - 1] = a1_v[ys[k - 1][GY]].astype(BF16)
        third.append(send(c1_s.at[k - 1], c1_r.at[k - 1], ys[k - 1]))
    for k in (2, 1, 3):
        c2_s[k - 1] = a2_v[xs[k - 1][GX]].astype(BF16)
        third.append(send(c2_s.at[k - 1], c2_r.at[k - 1], xs[k - 1]))
    for copy in sc:
        copy.wait_recv()
    sz_v[z] = (sy_v[0] + sy_v[1]) + (sy_v[2] + sy_v[3])
    sd = [send(sz_v.at[z], sz_v.at[z], zs[k]) for k in range(NZ - 1)]
    for copy in third:
        copy.wait_recv()
    fin1 = a1_v[y] + (c1_r[0].astype(F32) + c1_r[1].astype(F32) + c1_r[2].astype(F32))
    fin2 = a2_v[x] + (c2_r[0].astype(F32) + c2_r[1].astype(F32) + c2_r[2].astype(F32))
    for k in range(4):
        fin_v[k] = fin1[:, 128 * k : 128 * k + 128]
        fin_v[4 + k] = fin2[:, 128 * k : 128 * k + 128]
    d_s[...] = fin_v[...].astype(BF16)

    fourth = []
    for k in (4, 3, 5, 2, 6, 1, 7):
        fourth.append(send(d_s.at[zs[k - 1][GZ]], d_r.at[k - 1], zs[k - 1]))
    for copy in fourth:
        copy.wait_recv()
    whole = fin_v[z]
    for k in range(NZ - 1):
        whole = whole + d_r[k].astype(F32)
    e_v[z] = whole
    fifth = [send(e_v.at[z], e_v.at[z], zs[k - 1]) for k in (4, 3, 5, 2, 6, 1, 7)]
    for copy in sd:
        copy.wait_recv()
    gs = sz_v[0]
    for k in range(1, NZ):
        gs = gs + sz_v[k]
    gs_ref[...] = gs
    for copy in fifth:
        copy.wait_recv()
    for k in range(NZ):
        gh_ref[:, pl.ds(128 * k, 128)] = e_v[k]
    for copy in used:
        copy.wait_send()


def vmem(*items):
    return [pltpu.VMEM(s, t) for s, t in items]


def body(
    offer_attribute_matrix,
    kept_offers,
    expert_target,
    sequence_extent,
    behaviour_sequence,
    inner_projection_matrix,
    student_rating_vector,
    asking_matrix,
    lookup_matrix,
    content_matrix,
    expert_rating_vector,
):
    v_row = student_rating_vector.reshape(1, 1024)
    grad_hidden, grad_score = pl.pallas_call(
        whole_kernel,
        out_shape=[jax.ShapeDtypeStruct((32, 1024), F32), jax.ShapeDtypeStruct((8, 128), F32)],
        in_specs=[pl.BlockSpec(memory_space=pl.ANY)] * 11,
        out_specs=[pl.BlockSpec(memory_space=pltpu.VMEM)] * 2,
        scratch_shapes=[
            *vmem(*[((2, 4, 32, 1024), BF16)] * 4, *[((2, 4, 128, 512), BF16)] * 4),
            pltpu.VMEM((4, 2, 8, 128), jnp.int32),
            pltpu.SMEM((64, 128), jnp.int32),
            *vmem(
                ((4, 1024, 512), BF16),
                ((4, 512, 512), BF16),
                ((4, 16, 512), BF16),
                ((4, 512, 256), BF16),
                ((4, 2, 8, 128), F32),
                ((4, 32), jnp.int32),
                ((4, 6), jnp.int32),
                ((1, 4), jnp.int32),
                ((1, 1024), BF16),
                ((1, 512), BF16),
                ((4, 128, 1024), BF16),
                ((1024, 1024), BF16),
                ((512, 512), BF16),
                ((512, 1024), F32),
                ((512, 128), F32),
                ((1024, 512), BF16),
                ((32, 1024), F32),
                ((512, 1024), BF16),
                ((8, 8, 128), F32),
                ((16, 32, 1024), BF16),
                ((16, 32, 1024), BF16),
                ((16, 32, 1024), F32),
                *[((3, 4, 32, 512), BF16)] * 4,
                *[((4, 32, 512), F32)] * 2,
                *[((3, 32, 512), BF16)] * 4,
                ((8, 32, 128), F32),
                ((8, 32, 128), BF16),
                ((7, 32, 128), BF16),
                ((8, 32, 128), F32),
                ((2, 8, 128), F32),
                ((4, 8, 128), F32),
                ((4, 8, 128), F32),
                ((8, 8, 128), F32),
            ),
            pltpu.SemaphoreType.DMA((160,)),
            pltpu.SemaphoreType.DMA((160,)),
            pltpu.SemaphoreType.DMA((24,)),
        ],
        compiler_params=pltpu.CompilerParams(
            collective_id=0, has_side_effects=True, vmem_limit_bytes=63 * 2**20
        ),
        name="distillation_backward",
    )(
        offer_attribute_matrix, kept_offers, expert_target, sequence_extent.reshape(1, 4),
        inner_projection_matrix, v_row, behaviour_sequence,
        asking_matrix[0], lookup_matrix[0], content_matrix[0], expert_rating_vector,
    )
    return grad_hidden, grad_score.reshape(1024)


def solution(mesh):
    torus = Mesh(mesh.devices.reshape(mesh.shape["group"], NX, NY, 2), GROUP_SHARD)
    return jax.shard_map(
        body,
        mesh=torus,
        in_specs=(
            P(GROUP_SHARD, None, None),
            P(GROUP_SHARD, None),
            P(GROUP_SHARD, None),
            P(GROUP_SHARD),
            P(GROUP_SHARD, None, None),
            P(),
            P(),
            P(SHARD, None, None),
            P(SHARD, None, None),
            P(SHARD, None, None),
            P(SHARD, None),
        ),
        out_specs=(P(SHARD, None), P()),
        check_vma=False,
    )
```

```python
import functools

import jax
import jax.numpy as jnp
from jax import lax
from jax.experimental import pallas as pl
from jax.experimental.pallas import tpu as pltpu
from jax.sharding import Mesh
from jax.sharding import PartitionSpec as P

MESH = pl.DeviceIdType.MESH
F32 = jnp.float32
BF16 = jnp.bfloat16
HEADS = 8
GZ, GX, GY, GC = "group", "shard_0", "shard_1", "shard_2"
SHARD = (GX, GY, GC)
GROUP_SHARD = (GZ, GX, GY, GC)
NX, NY, NZ = 4, 4, 8
SLICE = 80
SPLIT = SLICE * NZ
NT = (((1,), (1,)), ((), ()))
TN = (((0,), (0,)), ((), ()))


def dot(a, b, dims=(((1,), (0,)), ((), ()))):
    return lax.dot_general(a, b, dims, preferred_element_type=F32)


class Sent:
    def __init__(self, copy):
        self.copy, self.arrived = copy, False
        copy.start()

    def wait_recv(self):
        if not self.arrived:
            self.copy.wait_recv()
        self.arrived = True

    def wait_send(self):
        self.copy.wait_send()


def at(axis, step, size):
    return {axis: lax.rem(lax.axis_index(axis) + (step % size), size)}


def whole_kernel(
    x_ref, kept_in, target_in, extent_in, w1_ref, v_in, hist_ref, wq_ref, wk_ref, wv_ref, rat_in,
    gh_ref, gs_ref,
    sel0, sel1, sel2, sel3, hist0, hist1, hist2, hist3,
    meta_all, meta_s, wq_all, wk_all, wr_all, wide_v, acc_v,
    kept_ref, target_ref, extent_ref, v_ref, rat_ref,
    x_v, w1_v, wv_v, hid_v, st_v, xt_v, sum_v,
    hg_v, t_v, ga_s, ga_r, own_v, b1_s, b1_r, b2_s, b2_r, a1_v, a2_v,
    c1_s, c1_r, c2_s, c2_r, fin_v, d_s, d_r, e_v, s0_v, sx_v, sy_v, sz_v, send_sem, recv_sem, load_sem,
):
    sel_p, hist_p = (sel0, sel1, sel2, sel3), (hist0, hist1, hist2, hist3)
    x, y, z, c = (lax.axis_index(a) for a in (GX, GY, GZ, GC))
    other = {GC: 1 - c}
    used = []

    def send(src, dst, device):
        k = len(used)
        used.append(
            Sent(
                pltpu.make_async_remote_copy(
                    src_ref=src, dst_ref=dst, send_sem=send_sem.at[k], recv_sem=recv_sem.at[k],
                    device_id=device, device_id_type=MESH,
                )
            )
        )
        return used[-1]

    loads = []

    def load(src, dst):
        copy = pltpu.make_async_copy(src, dst, load_sem.at[len(loads)])
        copy.start()
        loads.append(copy)
        return copy

    load_small = [
        load(src, dst)
        for src, dst in (
            (target_in, target_ref), (extent_in, extent_ref), (kept_in, kept_ref), (rat_in, rat_ref),
            (v_in, v_ref),
        )
    ]
    load_x = load(x_ref, x_v)
    load_wv = load(wv_ref, wv_v)
    load_own = [load(hist_ref, hist0.at[0]), load(wq_ref, wq_all.at[0]), load(wk_ref, wk_all.at[0])]
    load_w1 = load(w1_ref, w1_v)

    xs = [at(GX, k, NX) for k in (1, 2, 3)]
    ys = [at(GY, k, NY) for k in (1, 2, 3)]
    zs = [at(GZ, k, NZ) for k in range(1, NZ)]
    diag = [{**d, **other} for d in xs]
    peers = [*xs, *ys, *zs, *diag, other]
    barrier = pltpu.get_barrier_semaphore()
    for peer in peers:
        pl.semaphore_signal(barrier, inc=1, device_id=peer, device_id_type=MESH)
    pl.semaphore_wait(barrier, len(peers))

    def zrows(step, start=0, size=SLICE):
        plane = lax.rem(z + (step % NZ), NZ)
        return pl.ds(pl.multiple_of(plane * SLICE + start, 16), size)

    half = SLICE // 32 * 16
    more = SLICE - half
    tail = (1024 - SPLIT) // 2
    xR, xL, yR, yL, zR, zL = xs[0], xs[2], ys[0], ys[2], zs[0], zs[6]

    zsR = send(wq_ref.at[zrows(0)], wq_all.at[2, zrows(0)], yR)
    zsL = send(wq_ref.at[zrows(0)], wq_all.at[1, zrows(0)], yL)

    def two(h):
        return pl.ds(2 * h, 2)

    def x_hist(h, device, slot):
        return send(hist_ref.at[two(h)], hist_p[slot].at[0, two(h)], device)

    def x_sel(h, device, slot):
        return send(sel0.at[0, two(h)], sel_p[slot].at[0, two(h)], device)

    def y_k(h, device, slot):
        rows = pl.ds(256 * h, 256)
        return send(wk_ref.at[rows], wk_all.at[slot, rows], device)

    def y_q(h, device, slot):
        rows = pl.ds(SPLIT + tail * h, tail)
        return send(wq_ref.at[rows], wq_all.at[slot, rows], device)

    histR, histL = {0: x_hist(0, xR, 2)}, {1: x_hist(1, xL, 1)}
    ykR, ykL = {0: y_k(0, yR, 2)}, {1: y_k(1, yL, 1)}
    for copy in load_small:
        copy.wait()
    bits = jnp.sum(jnp.left_shift(jnp.int32(1), target_ref[...]), axis=1, keepdims=True)
    meta_all[0, 0] = jnp.zeros((8, 128), jnp.int32)
    meta_all[0, 0, pl.ds(0, 4), :] = jnp.broadcast_to(bits, (4, 128))
    meta_all[0, 0, pl.ds(4, 1), pl.ds(0, 4)] = extent_ref[...]
    metaR = send(meta_all.at[0, 0], meta_all.at[2, 0], xR)
    metaL = send(meta_all.at[0, 0], meta_all.at[1, 0], xL)
    meta2 = send(meta_all.at[0, 0], meta_all.at[3, 0], xs[1])
    meta_on = [send(meta_all.at[0, 0], meta_all.at[0, 1], other)]

    load_x.wait()
    for r in range(4):
        onehot = (
            lax.broadcasted_iota(jnp.int32, (128, 32), 0) == kept_ref[pl.ds(r, 1), :]
        ).astype(F32).astype(BF16)
        sel0[0, r] = dot(onehot, x_v[r], TN).astype(BF16)
    selR, selL = {0: x_sel(0, xR, 2)}, {1: x_sel(1, xL, 1)}

    load_wv.wait()
    head_wide = lax.broadcasted_iota(jnp.int32, (16, 512), 1) // 64
    row_of = lax.broadcasted_iota(jnp.int32, (16, 512), 0)
    rating = jnp.where(head_wide == row_of, rat_ref[...].astype(F32), 0.0).astype(BF16)
    wr_all[0] = dot(rating, wv_v[...], NT).astype(BF16)
    wrR = send(wr_all.at[0], wr_all.at[2], yR)
    wrL = send(wr_all.at[0], wr_all.at[1], yL)
    wr2 = send(wr_all.at[0], wr_all.at[3], ys[1])

    zsR.wait_recv()
    zsL.wait_recv()
    gA, gB = pl.ds(1, 2), pl.ds(3, 1)

    def z_send(group, step, device, start=0, size=SLICE):
        rows = zrows(step, start, size)
        return send(wq_all.at[group, rows], wq_all.at[group, rows], device)

    aR, aL = [z_send(gA, 0, zR)], [z_send(gA, 0, zL)]
    zs2R = send(wq_all.at[2, zrows(0, 0, half)], wq_all.at[3, zrows(0, 0, half)], yR)
    zs2L = send(wq_all.at[1, zrows(0, half, more)], wq_all.at[3, zrows(0, half, more)], yL)
    yqR, yqL = {0: y_q(0, yR, 2)}, {1: y_q(1, yL, 1)}
    histR[1], histL[0] = x_hist(1, xR, 2), x_hist(0, xL, 1)
    selR[1], selL[0] = x_sel(1, xR, 2), x_sel(0, xL, 1)
    ykR[1], ykL[0] = y_k(1, yR, 2), y_k(0, yL, 1)
    yqR[1], yqL[0] = y_q(1, yR, 2), y_q(0, yL, 1)
    on = {0: [send(hist_ref, hist0.at[1], other), send(sel0.at[0], sel0.at[1], other)], 1: [], 2: [], 3: []}

    def tower(r):
        rows = pl.ds(128 * r, 128)
        block = x_v[r]
        scores = jnp.zeros((128, 1), F32)
        for q in range(4):
            cols = pl.ds(256 * q, 256)
            hidden = jnp.maximum(dot(block, w1_v[:, cols]), 0.0)
            hid_v[rows, cols] = hidden
            scores = scores + jnp.sum(hidden * v_ref[:, cols].astype(F32), axis=1, keepdims=True)
        weights = jnp.exp(scores)
        st_v[rows, :] = jnp.broadcast_to(weights / jnp.sum(weights, axis=0, keepdims=True), (128, 128))
        xt_v[:, rows] = block.T

    load_w1.wait()
    tower(0)

    def x_across(refs, slot, h, arrived):
        arrived.wait_recv()
        on[slot].append(send(refs[slot].at[0, two(h)], refs[slot].at[1, two(h)], other))

    def x_forward(refs, h, arrived):
        arrived.wait_recv()
        device, slot = (xR, 2) if h == 0 else (xL, 1)
        sent = send(refs[slot].at[0, two(h)], refs[3].at[0, two(h)], device)
        x_across(refs, slot, h, arrived)
        return sent

    def y_forward(h, ak, aq):
        device, slot = (yR, 2) if h == 0 else (yL, 1)
        ak.wait_recv()
        rows = pl.ds(256 * h, 256)
        send(wk_all.at[slot, rows], wk_all.at[3, rows], device)
        aq.wait_recv()
        rows = pl.ds(SPLIT + tail * h, tail)
        send(wq_all.at[slot, rows], wq_all.at[3, rows], device)

    metaR.wait_recv()
    metaL.wait_recv()
    meta_on.append(send(meta_all.at[2, 0], meta_all.at[2, 1], other))
    meta_on.append(send(meta_all.at[1, 0], meta_all.at[1, 1], other))
    zs2R.wait_recv()
    zs2L.wait_recv()
    bR, bL = [z_send(gB, 0, zR)], [z_send(gB, 0, zL)]
    tower(1)
    hist2R = x_forward(hist_p, 0, histR[0])
    hist2L = x_forward(hist_p, 1, histL[1])
    aR[0].wait_recv()
    aR.append(z_send(gA, -1, zR))
    aL[0].wait_recv()
    aL.append(z_send(gA, 1, zL))
    tower(2)
    sel2R = x_forward(sel_p, 0, selR[0])
    sel2L = x_forward(sel_p, 1, selL[1])
    meta2.wait_recv()
    meta_on.append(send(meta_all.at[3, 0], meta_all.at[3, 1], other))
    bR[0].wait_recv()
    bR.append(z_send(gB, -1, zR))
    bL[0].wait_recv()
    bL.append(z_send(gB, 1, zL))
    tower(3)
    y_forward(0, ykR[0], yqR[0])
    y_forward(1, ykL[1], yqL[1])
    for copy in meta_on:
        copy.wait_recv()
    info = [
        load(meta_all.at[k // 2, k % 2], meta_s.at[pl.ds(8 * k, 8)]) for k in range(8)
    ]
    acc_v[...] = jnp.zeros_like(acc_v)

    head_of = lax.broadcasted_iota(jnp.int32, (32, 512), 1) // 64
    slot_row = lax.broadcasted_iota(jnp.int32, (128, 256), 0)
    out_row = lax.broadcasted_iota(jnp.int32, (8, 128), 0)

    def ranked(d, p):
        step = jnp.where(d == 3, 2, jnp.where(d == 2, 3, jnp.where(d == 1, 1, 0)))
        expert = (x * 4 + lax.rem(y + step, 4)) * 2 + c
        places = []
        for core in range(2):
            base = 16 * p + 8 * core
            seen = jnp.int32(0)
            ids, found = [jnp.int32(0)] * 2, [jnp.int32(0)] * 2
            for i in range(4):
                here = lax.shift_right_logical(meta_s[base + i, 0], expert) & 1
                for j in range(2):
                    hit = jnp.where(seen == j, here, 0)
                    ids[j] = ids[j] + i * hit
                    found[j] = found[j] + hit
                seen = seen + here
            places += [(core, ids[j], found[j]) for j in range(2)]
        rows = jnp.concatenate([sel_p[p][core, i] for core, i, _ in places], axis=0)
        queries = dot(rows, wq_all[d]).astype(BF16)
        slots = jnp.concatenate([hist_p[p][core, i] for core, i, _ in places], axis=0)
        keys = dot(slots, wk_all[d]).astype(BF16)
        worth = dot(slots, wide_v[d])
        for k, (core, i, found) in enumerate(places):
            length = meta_s[16 * p + 8 * core + 4, i]
            mine = queries[32 * k : 32 * k + 32]
            spread = jnp.concatenate(
                [jnp.where(head_of == h, mine, jnp.zeros_like(mine)) for h in range(HEADS)], axis=0
            )
            logits = dot(keys[128 * k : 128 * k + 128], spread, NT) * 0.125
            w = jnp.where(slot_row < length, jnp.exp(logits), 0.0)
            top = jnp.sum(w * worth[128 * k : 128 * k + 128], axis=0, keepdims=True)
            score = top / jnp.sum(w, axis=0, keepdims=True)
            score = score[:, :128] + score[:, 128:]
            score = score + pltpu.roll(score, 64, 1)
            score = score + pltpu.roll(score, 32, 1)
            mark = out_row == jnp.where(found == 1, i, -1)
            acc_v[p, core] = acc_v[p, core] + jnp.where(mark, score, 0.0)

    def widened(d):
        small = wr_all[d].astype(F32)
        wide = [jnp.broadcast_to(small[h : h + 1, :], (32, 512)) for h in range(HEADS)]
        wide_v[d] = jnp.concatenate(wide, axis=0).T.astype(BF16)

    def expert_run(low, high, groups):
        @pl.loop(low, high)
        def _(d):
            for p in groups:
                ranked(d, p)

    def arrived(*copies):
        for copy in copies:
            copy.wait_recv()

    for copy in (*info, *load_own):
        copy.wait()
    widened(0)
    arrived(*on[0])
    ranked(0, 0)
    aR[1].wait_recv()
    aR.append(z_send(gA, -2, zR))
    aL[1].wait_recv()
    aL.append(z_send(gA, 2, zL))
    bR[1].wait_recv()
    bR.append(z_send(gB, -2, zR))
    bL[1].wait_recv()
    bL.append(z_send(gB, 2, zL))
    x_across(hist_p, 2, 1, histR[1])
    x_across(hist_p, 1, 0, histL[0])
    x_across(sel_p, 2, 1, selR[1])
    x_across(sel_p, 1, 0, selL[0])
    arrived(wrR, wrL, wr2)

    @pl.loop(1, 4)
    def _(d):
        widened(d)

    aR[2].wait_recv()
    aR.append(z_send(gA, -3, zR, 0, half))
    aL[2].wait_recv()
    aL.append(z_send(gA, 3, zL, half, more))
    arrived(*on[1], *on[2])
    ranked(0, 1)
    ranked(0, 2)
    bR[2].wait_recv()
    bR.append(z_send(gB, -3, zR, 0, half))
    bL[2].wait_recv()
    bL.append(z_send(gB, 3, zL, half, more))
    x_across(hist_p, 3, 0, hist2R)
    x_across(hist_p, 3, 1, hist2L)
    x_across(sel_p, 3, 0, sel2R)
    x_across(sel_p, 3, 1, sel2L)
    arrived(*ykR.values(), *ykL.values(), *yqR.values(), *yqL.values(), *aR, *aL)
    arrived(*on[1], *on[2])
    expert_run(1, 3, range(3))
    arrived(*on[3])
    expert_run(0, 3, (3,))
    arrived(*used)
    expert_run(3, 4, range(4))

    back = []
    slot_of = {1: 1, 2: 3, 3: 2}
    for k in (1, 2, 3):
        s = slot_of[k]
        back.append(send(acc_v.at[s, 0], t_v.at[2 * s], xs[k - 1]))
        back.append(send(acc_v.at[s, 1], t_v.at[2 * s + 1], diag[k - 1]))
    back.append(send(acc_v.at[0, 1], t_v.at[1], other))
    t_v[0] = acc_v[0, 0]
    for copy in back:
        copy.wait_recv()
    teacher = t_v[0]
    for k in range(1, 8):
        teacher = teacher + t_v[k]
    live = lax.broadcasted_iota(jnp.int32, (8, 128), 1) < 32
    risen = jnp.where(live, jnp.exp(teacher / 6.0), 0.0)
    t_v[0] = risen / jnp.sum(risen, axis=1, keepdims=True)

    for r in range(4):
        rows = pl.ds(128 * r, 128)
        spots = lax.broadcasted_iota(jnp.int32, (128, 32), 0) == kept_ref[pl.ds(r, 1), :]
        aim = jnp.sum(jnp.where(spots, t_v[0, pl.ds(r, 1), pl.ds(0, 32)], 0.0), axis=1, keepdims=True)
        grad = st_v[rows, pl.ds(0, 1)] - aim
        for q in range(4):
            cols = pl.ds(256 * q, 256)
            hidden = hid_v[rows, cols]
            hg_v[rows, cols] = jnp.where(hidden > 0.0, grad * v_ref[:, cols].astype(F32), 0.0).astype(BF16)
            sum_v[pl.ds(8 * r, 8), cols] = jnp.sum((grad * hidden).reshape(16, 8, 256), axis=0)
    row = jnp.sum(sum_v[...], axis=0, keepdims=True)
    for k in range(8):
        s0_v[0, pl.ds(k, 1), :] = row[:, 128 * k : 128 * k + 128]
    sa = send(s0_v.at[0], s0_v.at[1], other)

    core = []

    def rows_of(k, side):
        return jnp.concatenate(
            [xt_v[pl.ds(pl.multiple_of(64 * (4 * k + j) + 32 * side, 32), 32), :] for j in range(4)], axis=0
        )

    for k in range(4):
        ga_s[pl.ds(4 * k, 4)] = dot(rows_of(k, 1 - c), hg_v[...]).astype(BF16).reshape(4, 32, 1024)
        core.append(send(ga_s.at[pl.ds(4 * k, 4)], ga_r.at[pl.ds(4 * k, 4)], other))
    for k in range(4):
        own_v[pl.ds(4 * k, 4)] = dot(rows_of(k, c), hg_v[...]).reshape(4, 32, 1024)
    for k in range(4):
        core[k].wait_recv()
        blocks = pl.ds(4 * k, 4)
        own_v[blocks] = own_v[blocks] + ga_r[blocks].astype(F32)
    sa.wait_recv()
    sx_v[x] = s0_v[0] + s0_v[1]

    n1, n2 = pl.ds(0, 512), pl.ds(512, 512)

    def along_x(side, h):
        return own_v[pl.ds(4 * side[GX] + 2 * h, 2), :, n1]

    def along_y(side, h):
        return jnp.stack([own_v[4 * (2 * h + j) + side[GY], :, n2] for j in range(2)])

    ways = ((along_x, xs, b1_s, b1_r), (along_y, ys, b2_s, b2_r))
    relay, direct = [], []
    for part, sides, out, into in ways:
        for h, device in ((0, sides[0]), (1, sides[2])):
            out[0, pl.ds(2 * h, 2)] = part(sides[1], h).astype(BF16)
            relay.append(send(out.at[0, pl.ds(2 * h, 2)], into.at[0, pl.ds(2 * h, 2)], device))
    sb = [send(sx_v.at[x], sx_v.at[x], xs[k]) for k in range(3)]
    for part, sides, out, into in ways:
        for h, device in ((1, sides[0]), (0, sides[2])):
            k = 2 - h
            out[k, pl.ds(2 * h, 2)] = part(device, h).astype(BF16)
            direct.append(send(out.at[k, pl.ds(2 * h, 2)], into.at[k, pl.ds(2 * h, 2)], device))
    for n, (part, sides, out, into) in enumerate(ways):
        for h, device in ((0, sides[0]), (1, sides[2])):
            relay[2 * n + h].wait_recv()
            k = 1 + h
            rows = pl.ds(2 * h, 2)
            out[k, rows] = (part(device, h) + into[0, rows].astype(F32)).astype(BF16)
            direct.append(send(out.at[k, rows], into.at[k, rows], device))
    for copy in sb:
        copy.wait_recv()
    sy_v[y] = (sx_v[0] + sx_v[1]) + (sx_v[2] + sx_v[3])
    sc = [send(sy_v.at[y], sy_v.at[y], ys[k]) for k in range(3)]
    for copy in direct:
        copy.wait_recv()
    a1_v[...] = own_v[pl.ds(4 * x, 4), :, n1] + (b1_r[1].astype(F32) + b1_r[2].astype(F32))
    for j in range(4):
        a2_v[j] = own_v[4 * j + y, :, n2] + (b2_r[1, j].astype(F32) + b2_r[2, j].astype(F32))
    third = []
    for k in (2, 1, 3):
        c1_s[k - 1] = a1_v[ys[k - 1][GY]].astype(BF16)
        third.append(send(c1_s.at[k - 1], c1_r.at[k - 1], ys[k - 1]))
    for k in (2, 1, 3):
        c2_s[k - 1] = a2_v[xs[k - 1][GX]].astype(BF16)
        third.append(send(c2_s.at[k - 1], c2_r.at[k - 1], xs[k - 1]))
    for copy in sc:
        copy.wait_recv()
    sz_v[z] = (sy_v[0] + sy_v[1]) + (sy_v[2] + sy_v[3])
    sd = [send(sz_v.at[z], sz_v.at[z], zs[k]) for k in range(NZ - 1)]
    for copy in third:
        copy.wait_recv()
    fin1 = a1_v[y] + (c1_r[0].astype(F32) + c1_r[1].astype(F32) + c1_r[2].astype(F32))
    fin2 = a2_v[x] + (c2_r[0].astype(F32) + c2_r[1].astype(F32) + c2_r[2].astype(F32))
    for k in range(4):
        fin_v[k] = fin1[:, 128 * k : 128 * k + 128]
        fin_v[4 + k] = fin2[:, 128 * k : 128 * k + 128]
    d_s[...] = fin_v[...].astype(BF16)

    fourth = []
    for k in (4, 3, 5, 2, 6, 1, 7):
        fourth.append(send(d_s.at[zs[k - 1][GZ]], d_r.at[k - 1], zs[k - 1]))
    for copy in fourth:
        copy.wait_recv()
    whole = fin_v[z]
    for k in range(NZ - 1):
        whole = whole + d_r[k].astype(F32)
    e_v[z] = whole
    fifth = [send(e_v.at[z], e_v.at[z], zs[k - 1]) for k in (4, 3, 5, 2, 6, 1, 7)]
    for copy in sd:
        copy.wait_recv()
    gs = sz_v[0]
    for k in range(1, NZ):
        gs = gs + sz_v[k]
    gs_ref[...] = gs
    for copy in fifth:
        copy.wait_recv()
    for k in range(NZ):
        gh_ref[:, pl.ds(128 * k, 128)] = e_v[k]
    for copy in used:
        copy.wait_send()


def vmem(*items):
    return [pltpu.VMEM(s, t) for s, t in items]


def body(
    offer_attribute_matrix,
    kept_offers,
    expert_target,
    sequence_extent,
    behaviour_sequence,
    inner_projection_matrix,
    student_rating_vector,
    asking_matrix,
    lookup_matrix,
    content_matrix,
    expert_rating_vector,
):
    v_row = student_rating_vector.reshape(1, 1024)
    grad_hidden, grad_score = pl.pallas_call(
        whole_kernel,
        out_shape=[jax.ShapeDtypeStruct((32, 1024), F32), jax.ShapeDtypeStruct((8, 128), F32)],
        in_specs=[pl.BlockSpec(memory_space=pl.ANY)] * 11,
        out_specs=[pl.BlockSpec(memory_space=pltpu.VMEM)] * 2,
        scratch_shapes=[
            *vmem(*[((2, 4, 32, 1024), BF16)] * 4, *[((2, 4, 128, 512), BF16)] * 4),
            pltpu.VMEM((4, 2, 8, 128), jnp.int32),
            pltpu.SMEM((64, 128), jnp.int32),
            *vmem(
                ((4, 1024, 512), BF16),
                ((4, 512, 512), BF16),
                ((4, 16, 512), BF16),
                ((4, 512, 256), BF16),
                ((4, 2, 8, 128), F32),
                ((4, 32), jnp.int32),
                ((4, 6), jnp.int32),
                ((1, 4), jnp.int32),
                ((1, 1024), BF16),
                ((1, 512), BF16),
                ((4, 128, 1024), BF16),
                ((1024, 1024), BF16),
                ((512, 512), BF16),
                ((512, 1024), F32),
                ((512, 128), F32),
                ((1024, 512), BF16),
                ((32, 1024), F32),
                ((512, 1024), BF16),
                ((8, 8, 128), F32),
                ((16, 32, 1024), BF16),
                ((16, 32, 1024), BF16),
                ((16, 32, 1024), F32),
                *[((3, 4, 32, 512), BF16)] * 4,
                *[((4, 32, 512), F32)] * 2,
                *[((3, 32, 512), BF16)] * 4,
                ((8, 32, 128), F32),
                ((8, 32, 128), BF16),
                ((7, 32, 128), BF16),
                ((8, 32, 128), F32),
                ((2, 8, 128), F32),
                ((4, 8, 128), F32),
                ((4, 8, 128), F32),
                ((8, 8, 128), F32),
            ),
            pltpu.SemaphoreType.DMA((160,)),
            pltpu.SemaphoreType.DMA((160,)),
            pltpu.SemaphoreType.DMA((24,)),
        ],
        compiler_params=pltpu.CompilerParams(
            collective_id=0, has_side_effects=True, vmem_limit_bytes=63 * 2**20
        ),
        name="distillation_backward",
    )(
        offer_attribute_matrix, kept_offers, expert_target, sequence_extent.reshape(1, 4),
        inner_projection_matrix, v_row, behaviour_sequence,
        asking_matrix[0], lookup_matrix[0], content_matrix[0], expert_rating_vector,
    )
    return grad_hidden, grad_score.reshape(1024)


def solution(mesh):
    torus = Mesh(mesh.devices.reshape(mesh.shape["group"], NX, NY, 2), GROUP_SHARD)
    return jax.shard_map(
        body,
        mesh=torus,
        in_specs=(
            P(GROUP_SHARD, None, None),
            P(GROUP_SHARD, None),
            P(GROUP_SHARD, None),
            P(GROUP_SHARD),
            P(GROUP_SHARD, None, None),
            P(),
            P(),
            P(SHARD, None, None),
            P(SHARD, None, None),
            P(SHARD, None, None),
            P(SHARD, None),
        ),
        out_specs=(P(SHARD, None), P()),
        check_vma=False,
    )
```

```python
import functools

import jax
import jax.numpy as jnp
from jax import lax
from jax.experimental import pallas as pl
from jax.experimental.pallas import tpu as pltpu
from jax.sharding import Mesh
from jax.sharding import PartitionSpec as P

MESH = pl.DeviceIdType.MESH
F32 = jnp.float32
BF16 = jnp.bfloat16
HEADS = 8
GZ, GX, GY, GC = "group", "shard_0", "shard_1", "shard_2"
SHARD = (GX, GY, GC)
GROUP_SHARD = (GZ, GX, GY, GC)
NX, NY, NZ = 4, 4, 8
SLICE = 64
SPLIT = SLICE * NZ
NT = (((1,), (1,)), ((), ()))
TN = (((0,), (0,)), ((), ()))


def dot(a, b, dims=(((1,), (0,)), ((), ()))):
    return lax.dot_general(a, b, dims, preferred_element_type=F32)


class Sent:
    def __init__(self, copy):
        self.copy, self.arrived = copy, False
        copy.start()

    def wait_recv(self):
        if not self.arrived:
            self.copy.wait_recv()
        self.arrived = True

    def wait_send(self):
        self.copy.wait_send()


def at(axis, step, size):
    return {axis: lax.rem(lax.axis_index(axis) + (step % size), size)}


def whole_kernel(
    x_ref, kept_in, target_in, extent_in, w1_ref, v_in, hist_ref, wq_ref, wk_ref, wv_ref, rat_in,
    gh_ref, gs_ref,
    sel0, sel1, sel2, sel3, hist0, hist1, hist2, hist3,
    meta_all, meta_s, wq_all, wk_all, wr_all, wide_v, acc_v,
    kept_ref, target_ref, extent_ref, v_rows, v_ref, rat_ref,
    x_v, w1_v, wv_v, hid_v, st_v, xt_v, sum_v,
    hg_v, t_v, ga_s, ga_r, own_v, b1_s, b1_r, b2_s, b2_r, a1_v, a2_v,
    c1_s, c1_r, c2_s, c2_r, fin_v, d_s, d_r, e_v, s0_v, sx_v, sy_v, sz_v, send_sem, recv_sem, load_sem,
):
    sel_p, hist_p = (sel0, sel1, sel2, sel3), (hist0, hist1, hist2, hist3)
    x, y, z, c = (lax.axis_index(a) for a in (GX, GY, GZ, GC))
    other = {GC: 1 - c}
    used = []

    def send(src, dst, device):
        k = len(used)
        used.append(
            Sent(
                pltpu.make_async_remote_copy(
                    src_ref=src, dst_ref=dst, send_sem=send_sem.at[k], recv_sem=recv_sem.at[k],
                    device_id=device, device_id_type=MESH,
                )
            )
        )
        return used[-1]

    loads = []

    def load(src, dst):
        copy = pltpu.make_async_copy(src, dst, load_sem.at[len(loads)])
        copy.start()
        loads.append(copy)
        return copy

    load_small = [
        load(src, dst)
        for src, dst in (
            (target_in, target_ref), (extent_in, extent_ref), (kept_in, kept_ref), (rat_in, rat_ref),
            (v_in, v_rows),
        )
    ]
    load_x = load(x_ref, x_v)
    load_wv = load(wv_ref, wv_v)
    load_own = [load(hist_ref, hist0.at[0]), load(wq_ref, wq_all.at[0]), load(wk_ref, wk_all.at[0])]
    load_w1 = load(w1_ref, w1_v)

    xs = [at(GX, k, NX) for k in (1, 2, 3)]
    ys = [at(GY, k, NY) for k in (1, 2, 3)]
    zs = [at(GZ, k, NZ) for k in range(1, NZ)]
    diag = [{**d, **other} for d in xs]
    peers = [*xs, *ys, *zs, *diag, other]
    barrier = pltpu.get_barrier_semaphore()
    for peer in peers:
        pl.semaphore_signal(barrier, inc=1, device_id=peer, device_id_type=MESH)
    pl.semaphore_wait(barrier, len(peers))

    def zrows(step, start=0, size=SLICE):
        plane = lax.rem(z + (step % NZ), NZ)
        return pl.ds(pl.multiple_of(plane * SLICE + start, 16), size)

    half = SLICE // 32 * 16
    more = SLICE - half
    tail = (1024 - SPLIT) // 2
    xR, xL, yR, yL, zR, zL = xs[0], xs[2], ys[0], ys[2], zs[0], zs[6]

    zsR = send(wq_ref.at[zrows(0)], wq_all.at[2, zrows(0)], yR)
    zsL = send(wq_ref.at[zrows(0)], wq_all.at[1, zrows(0)], yL)

    def two(h):
        return pl.ds(2 * h, 2)

    def x_hist(h, device, slot):
        return send(hist_ref.at[two(h)], hist_p[slot].at[0, two(h)], device)

    def x_sel(h, device, slot):
        return send(sel0.at[0, two(h)], sel_p[slot].at[0, two(h)], device)

    def y_k(h, device, slot):
        rows = pl.ds(256 * h, 256)
        return send(wk_ref.at[rows], wk_all.at[slot, rows], device)

    def y_q(h, device, slot):
        rows = pl.ds(SPLIT + tail * h, tail)
        return send(wq_ref.at[rows], wq_all.at[slot, rows], device)

    histR, histL = {0: x_hist(0, xR, 2)}, {1: x_hist(1, xL, 1)}
    ykR, ykL = {0: y_k(0, yR, 2)}, {1: y_k(1, yL, 1)}
    for copy in load_small:
        copy.wait()
    bits = jnp.sum(jnp.left_shift(jnp.int32(1), target_ref[...]), axis=1, keepdims=True)
    meta_all[0, 0] = jnp.zeros((8, 128), jnp.int32)
    meta_all[0, 0, pl.ds(0, 4), :] = jnp.broadcast_to(bits, (4, 128))
    meta_all[0, 0, pl.ds(4, 1), pl.ds(0, 4)] = extent_ref[...]
    metaR = send(meta_all.at[0, 0], meta_all.at[2, 0], xR)
    metaL = send(meta_all.at[0, 0], meta_all.at[1, 0], xL)
    meta2 = send(meta_all.at[0, 0], meta_all.at[3, 0], xs[1])
    meta_on = [send(meta_all.at[0, 0], meta_all.at[0, 1], other)]

    for k in range(8):
        v_ref[:, pl.ds(128 * k, 128)] = v_rows[...].astype(F32)[k : k + 1, :]

    load_x.wait()
    for r in range(4):
        onehot = (
            lax.broadcasted_iota(jnp.int32, (128, 32), 0) == kept_ref[pl.ds(r, 1), :]
        ).astype(F32).astype(BF16)
        sel0[0, r] = dot(onehot, x_v[r], TN).astype(BF16)
    selR, selL = {0: x_sel(0, xR, 2)}, {1: x_sel(1, xL, 1)}

    load_wv.wait()
    head_wide = lax.broadcasted_iota(jnp.int32, (16, 512), 1) // 64
    row_of = lax.broadcasted_iota(jnp.int32, (16, 512), 0)
    rating = jnp.where(head_wide == row_of, rat_ref[...].astype(F32), 0.0).astype(BF16)
    wr_all[0] = dot(rating, wv_v[...], NT).astype(BF16)
    wrR = send(wr_all.at[0], wr_all.at[2], yR)
    wrL = send(wr_all.at[0], wr_all.at[1], yL)
    wr2 = send(wr_all.at[0], wr_all.at[3], ys[1])

    zsR.wait_recv()
    zsL.wait_recv()
    gA, gB = pl.ds(1, 2), pl.ds(3, 1)

    def z_send(group, step, device, start=0, size=SLICE):
        rows = zrows(step, start, size)
        return send(wq_all.at[group, rows], wq_all.at[group, rows], device)

    aR, aL = [z_send(gA, 0, zR)], [z_send(gA, 0, zL)]
    zs2R = send(wq_all.at[2, zrows(0, 0, half)], wq_all.at[3, zrows(0, 0, half)], yR)
    zs2L = send(wq_all.at[1, zrows(0, half, more)], wq_all.at[3, zrows(0, half, more)], yL)
    yqR, yqL = {0: y_q(0, yR, 2)}, {1: y_q(1, yL, 1)}
    histR[1], histL[0] = x_hist(1, xR, 2), x_hist(0, xL, 1)
    selR[1], selL[0] = x_sel(1, xR, 2), x_sel(0, xL, 1)
    ykR[1], ykL[0] = y_k(1, yR, 2), y_k(0, yL, 1)
    yqR[1], yqL[0] = y_q(1, yR, 2), y_q(0, yL, 1)
    on = {0: [send(hist_ref, hist0.at[1], other), send(sel0.at[0], sel0.at[1], other)], 1: [], 2: [], 3: []}

    def tower(r):
        rows = pl.ds(128 * r, 128)
        block = x_v[r]
        scores = jnp.zeros((128, 1), F32)
        for q in range(4):
            cols = pl.ds(256 * q, 256)
            hidden = jnp.maximum(dot(block, w1_v[:, cols]), 0.0)
            hid_v[rows, cols] = hidden
            scores = scores + jnp.sum(hidden * v_ref[:, cols], axis=1, keepdims=True)
        weights = jnp.exp(scores)
        st_v[rows, :] = jnp.broadcast_to(weights / jnp.sum(weights, axis=0, keepdims=True), (128, 128))
        xt_v[:, rows] = block.T

    load_w1.wait()
    tower(0)

    def x_across(refs, slot, h, arrived):
        arrived.wait_recv()
        on[slot].append(send(refs[slot].at[0, two(h)], refs[slot].at[1, two(h)], other))

    def x_forward(refs, h, arrived):
        arrived.wait_recv()
        device, slot = (xR, 2) if h == 0 else (xL, 1)
        sent = send(refs[slot].at[0, two(h)], refs[3].at[0, two(h)], device)
        x_across(refs, slot, h, arrived)
        return sent

    def y_forward(h, ak, aq):
        device, slot = (yR, 2) if h == 0 else (yL, 1)
        ak.wait_recv()
        rows = pl.ds(256 * h, 256)
        send(wk_all.at[slot, rows], wk_all.at[3, rows], device)
        aq.wait_recv()
        rows = pl.ds(SPLIT + tail * h, tail)
        send(wq_all.at[slot, rows], wq_all.at[3, rows], device)

    metaR.wait_recv()
    metaL.wait_recv()
    meta_on.append(send(meta_all.at[2, 0], meta_all.at[2, 1], other))
    meta_on.append(send(meta_all.at[1, 0], meta_all.at[1, 1], other))
    zs2R.wait_recv()
    zs2L.wait_recv()
    bR, bL = [z_send(gB, 0, zR)], [z_send(gB, 0, zL)]
    meta2.wait_recv()
    meta_on.append(send(meta_all.at[3, 0], meta_all.at[3, 1], other))

    def z_step(group, rights, lefts, k):
        cut = k == 3
        rights[k - 1].wait_recv()
        rights.append(z_send(group, -k, zR, 0, half if cut else SLICE))
        lefts[k - 1].wait_recv()
        lefts.append(z_send(group, k, zL, half if cut else 0, more if cut else SLICE))

    tower(1)
    z_step(gA, aR, aL, 1)
    tower(2)
    z_step(gB, bR, bL, 1)
    tower(3)
    for copy in meta_on:
        copy.wait_recv()
    info = [
        load(meta_all.at[k // 2, k % 2], meta_s.at[pl.ds(8 * k, 8)]) for k in range(8)
    ]
    acc_v[...] = jnp.zeros_like(acc_v)

    head_of = lax.broadcasted_iota(jnp.int32, (32, 512), 1) // 64
    slot_row = lax.broadcasted_iota(jnp.int32, (128, 256), 0)
    out_row = lax.broadcasted_iota(jnp.int32, (8, 128), 0)

    def ranked(d, p):
        step = jnp.where(d == 3, 2, jnp.where(d == 2, 3, jnp.where(d == 1, 1, 0)))
        expert = (x * 4 + lax.rem(y + step, 4)) * 2 + c
        places = []
        for core in range(2):
            base = 16 * p + 8 * core
            seen = jnp.int32(0)
            ids, found = [jnp.int32(0)] * 2, [jnp.int32(0)] * 2
            for i in range(4):
                here = lax.shift_right_logical(meta_s[base + i, 0], expert) & 1
                for j in range(2):
                    hit = jnp.where(seen == j, here, 0)
                    ids[j] = ids[j] + i * hit
                    found[j] = found[j] + hit
                seen = seen + here
            places += [(core, ids[j], found[j]) for j in range(2)]
        rows = jnp.concatenate([sel_p[p][core, i] for core, i, _ in places], axis=0)
        queries = dot(rows, wq_all[d]).astype(BF16)
        slots = jnp.concatenate([hist_p[p][core, i] for core, i, _ in places], axis=0)
        keys = dot(slots, wk_all[d]).astype(BF16)
        worth = dot(slots, wide_v[d])
        for k, (core, i, found) in enumerate(places):
            length = meta_s[16 * p + 8 * core + 4, i]
            mine = queries[32 * k : 32 * k + 32]
            spread = jnp.concatenate(
                [jnp.where(head_of == h, mine, jnp.zeros_like(mine)) for h in range(HEADS)], axis=0
            )
            logits = dot(keys[128 * k : 128 * k + 128], spread, NT) * 0.125
            w = jnp.where(slot_row < length, jnp.exp(logits), 0.0)
            top = jnp.sum(w * worth[128 * k : 128 * k + 128], axis=0, keepdims=True)
            score = top / jnp.sum(w, axis=0, keepdims=True)
            score = score[:, :128] + score[:, 128:]
            score = score + pltpu.roll(score, 64, 1)
            score = score + pltpu.roll(score, 32, 1)
            mark = out_row == jnp.where(found == 1, i, -1)
            acc_v[p, core] = acc_v[p, core] + jnp.where(mark, score, 0.0)

    def widened(d):
        small = wr_all[d].astype(F32)
        wide = [jnp.broadcast_to(small[h : h + 1, :], (32, 512)) for h in range(HEADS)]
        wide_v[d] = jnp.concatenate(wide, axis=0).T.astype(BF16)

    def expert_run(low, high, groups):
        @pl.loop(low, high)
        def _(d):
            for p in groups:
                ranked(d, p)

    def arrived(*copies):
        for copy in copies:
            copy.wait_recv()

    for copy in (*info, *load_own):
        copy.wait()
    widened(0)
    arrived(*on[0])
    ranked(0, 0)
    z_step(gA, aR, aL, 2)
    arrived(wrR, wrL, wr2)

    @pl.loop(1, 4)
    def _(d):
        widened(d)

    z_step(gB, bR, bL, 2)
    hist2R = x_forward(hist_p, 0, histR[0])
    hist2L = x_forward(hist_p, 1, histL[1])
    sel2R = x_forward(sel_p, 0, selR[0])
    sel2L = x_forward(sel_p, 1, selL[1])
    y_forward(0, ykR[0], yqR[0])
    y_forward(1, ykL[1], yqL[1])
    z_step(gA, aR, aL, 3)
    x_across(hist_p, 2, 1, histR[1])
    x_across(hist_p, 1, 0, histL[0])
    x_across(sel_p, 2, 1, selR[1])
    x_across(sel_p, 1, 0, selL[0])
    arrived(*on[1], *on[2])
    ranked(0, 1)
    ranked(0, 2)
    z_step(gB, bR, bL, 3)
    x_across(hist_p, 3, 0, hist2R)
    x_across(hist_p, 3, 1, hist2L)
    x_across(sel_p, 3, 0, sel2R)
    x_across(sel_p, 3, 1, sel2L)
    arrived(*ykR.values(), *ykL.values(), *yqR.values(), *yqL.values(), *aR, *aL)
    expert_run(1, 3, range(3))
    arrived(*on[3])
    expert_run(0, 3, (3,))
    arrived(*used)
    back = []
    for p, k in ((3, 2), (1, 1), (2, 3), (0, 0)):
        ranked(3, p)
        if k:
            back.append(send(acc_v.at[p, 0], t_v.at[2 * p], xs[k - 1]))
        back.append(send(acc_v.at[p, 1], t_v.at[2 * p + 1], diag[k - 1] if k else other))
    t_v[0] = acc_v[0, 0]
    for copy in back:
        copy.wait_recv()
    teacher = t_v[0]
    for k in range(1, 8):
        teacher = teacher + t_v[k]
    live = lax.broadcasted_iota(jnp.int32, (8, 128), 1) < 32
    risen = jnp.where(live, jnp.exp(teacher / 6.0), 0.0)
    t_v[0] = risen / jnp.sum(risen, axis=1, keepdims=True)

    for r in range(4):
        rows = pl.ds(128 * r, 128)
        spots = lax.broadcasted_iota(jnp.int32, (128, 32), 0) == kept_ref[pl.ds(r, 1), :]
        aim = jnp.sum(jnp.where(spots, t_v[0, pl.ds(r, 1), pl.ds(0, 32)], 0.0), axis=1, keepdims=True)
        grad = st_v[rows, pl.ds(0, 1)] - aim
        for q in range(4):
            cols = pl.ds(256 * q, 256)
            hidden = hid_v[rows, cols]
            hg_v[rows, cols] = jnp.where(hidden > 0.0, grad * v_ref[:, cols], 0.0).astype(BF16)
            sum_v[pl.ds(8 * r, 8), cols] = jnp.sum((grad * hidden).reshape(16, 8, 256), axis=0)
    row = jnp.sum(sum_v[...], axis=0, keepdims=True)
    for k in range(8):
        s0_v[0, pl.ds(k, 1), :] = row[:, 128 * k : 128 * k + 128]
    sa = send(s0_v.at[0], s0_v.at[1], other)

    core = []

    def rows_of(k, side):
        return jnp.concatenate(
            [xt_v[pl.ds(pl.multiple_of(64 * (4 * k + j) + 32 * side, 32), 32), :] for j in range(4)], axis=0
        )

    n1, n2 = pl.ds(0, 512), pl.ds(512, 512)

    def along_x(side, h):
        return own_v[pl.ds(4 * side[GX] + 2 * h, 2), :, n1]

    def along_y(side, h):
        return jnp.stack([own_v[4 * (2 * h + j) + side[GY], :, n2] for j in range(2)])

    ways = ((along_x, xs, b1_s, b1_r), (along_y, ys, b2_s, b2_r))
    relay, direct = [], []

    def to_relay(part, sides, out, into):
        for h, device in ((0, sides[0]), (1, sides[2])):
            out[0, pl.ds(2 * h, 2)] = part(sides[1], h).astype(BF16)
            relay.append(send(out.at[0, pl.ds(2 * h, 2)], into.at[0, pl.ds(2 * h, 2)], device))

    def to_next(part, sides, out, into, h):
        k, device = 2 - h, sides[0] if h == 1 else sides[2]
        out[k, pl.ds(2 * h, 2)] = part(device, h).astype(BF16)
        direct.append(send(out.at[k, pl.ds(2 * h, 2)], into.at[k, pl.ds(2 * h, 2)], device))

    order = [xs[1][GX], xs[0][GX], xs[2][GX], x]
    for k in range(4):
        blocks = pl.ds(4 * order[k], 4)
        ga_s[blocks] = dot(rows_of(order[k], 1 - c), hg_v[...]).astype(BF16).reshape(4, 32, 1024)
        core.append(send(ga_s.at[blocks], ga_r.at[blocks], other))
    for k in range(4):
        own_v[pl.ds(4 * order[k], 4)] = dot(rows_of(order[k], c), hg_v[...]).reshape(4, 32, 1024)
    for k in range(4):
        core[k].wait_recv()
        blocks = pl.ds(4 * order[k], 4)
        own_v[blocks] = own_v[blocks] + ga_r[blocks].astype(F32)
        if k == 0:
            to_relay(*ways[0])
        if k in (1, 2):
            to_next(*ways[0], 2 - k)
    to_relay(*ways[1])
    to_next(*ways[1], 1)
    to_next(*ways[1], 0)
    sa.wait_recv()
    sx_v[x] = s0_v[0] + s0_v[1]
    sb = [send(sx_v.at[x], sx_v.at[x], xs[k]) for k in range(3)]
    for n, (part, sides, out, into) in enumerate(ways):
        for h, device in ((0, sides[0]), (1, sides[2])):
            relay[2 * n + h].wait_recv()
            k = 1 + h
            rows = pl.ds(2 * h, 2)
            out[k, rows] = (part(device, h) + into[0, rows].astype(F32)).astype(BF16)
            direct.append(send(out.at[k, rows], into.at[k, rows], device))
    for copy in sb:
        copy.wait_recv()
    sy_v[y] = (sx_v[0] + sx_v[1]) + (sx_v[2] + sx_v[3])
    sc = [send(sy_v.at[y], sy_v.at[y], ys[k]) for k in range(3)]
    for copy in direct:
        copy.wait_recv()
    a1_v[...] = own_v[pl.ds(4 * x, 4), :, n1] + (b1_r[1].astype(F32) + b1_r[2].astype(F32))
    for j in range(4):
        a2_v[j] = own_v[4 * j + y, :, n2] + (b2_r[1, j].astype(F32) + b2_r[2, j].astype(F32))
    third = []
    for k in (2, 1, 3):
        c1_s[k - 1] = a1_v[ys[k - 1][GY]].astype(BF16)
        third.append(send(c1_s.at[k - 1], c1_r.at[k - 1], ys[k - 1]))
    for k in (2, 1, 3):
        c2_s[k - 1] = a2_v[xs[k - 1][GX]].astype(BF16)
        third.append(send(c2_s.at[k - 1], c2_r.at[k - 1], xs[k - 1]))
    for copy in sc:
        copy.wait_recv()
    sz_v[z] = (sy_v[0] + sy_v[1]) + (sy_v[2] + sy_v[3])
    sd = [send(sz_v.at[z], sz_v.at[z], zs[k]) for k in range(NZ - 1)]
    for copy in third:
        copy.wait_recv()
    fin1 = a1_v[y] + (c1_r[0].astype(F32) + c1_r[1].astype(F32) + c1_r[2].astype(F32))
    fin2 = a2_v[x] + (c2_r[0].astype(F32) + c2_r[1].astype(F32) + c2_r[2].astype(F32))
    for k in range(4):
        fin_v[k] = fin1[:, 128 * k : 128 * k + 128]
        fin_v[4 + k] = fin2[:, 128 * k : 128 * k + 128]
    d_s[...] = fin_v[...].astype(BF16)

    fourth = []
    for k in (4, 3, 5, 2, 6, 1, 7):
        fourth.append(send(d_s.at[zs[k - 1][GZ]], d_r.at[k - 1], zs[k - 1]))
    for copy in fourth:
        copy.wait_recv()
    whole = fin_v[z]
    for k in range(NZ - 1):
        whole = whole + d_r[k].astype(F32)
    e_v[z] = whole
    fifth = [send(e_v.at[z], e_v.at[z], zs[k - 1]) for k in (4, 3, 5, 2, 6, 1, 7)]
    for copy in sd:
        copy.wait_recv()
    gs = sz_v[0]
    for k in range(1, NZ):
        gs = gs + sz_v[k]
    gs_ref[...] = gs
    for copy in fifth:
        copy.wait_recv()
    for k in range(NZ):
        gh_ref[:, pl.ds(128 * k, 128)] = e_v[k]
    for copy in used:
        copy.wait_send()


def vmem(*items):
    return [pltpu.VMEM(s, t) for s, t in items]


def body(
    offer_attribute_matrix,
    kept_offers,
    expert_target,
    sequence_extent,
    behaviour_sequence,
    inner_projection_matrix,
    student_rating_vector,
    asking_matrix,
    lookup_matrix,
    content_matrix,
    expert_rating_vector,
):
    v_row = student_rating_vector.reshape(8, 128)
    grad_hidden, grad_score = pl.pallas_call(
        whole_kernel,
        out_shape=[jax.ShapeDtypeStruct((32, 1024), F32), jax.ShapeDtypeStruct((8, 128), F32)],
        in_specs=[pl.BlockSpec(memory_space=pl.ANY)] * 11,
        out_specs=[pl.BlockSpec(memory_space=pltpu.VMEM)] * 2,
        scratch_shapes=[
            *vmem(*[((2, 4, 32, 1024), BF16)] * 4, *[((2, 4, 128, 512), BF16)] * 4),
            pltpu.VMEM((4, 2, 8, 128), jnp.int32),
            pltpu.SMEM((64, 128), jnp.int32),
            *vmem(
                ((4, 1024, 512), BF16),
                ((4, 512, 512), BF16),
                ((4, 16, 512), BF16),
                ((4, 512, 256), BF16),
                ((4, 2, 8, 128), F32),
                ((4, 32), jnp.int32),
                ((4, 6), jnp.int32),
                ((1, 4), jnp.int32),
                ((8, 128), BF16),
                ((1, 1024), F32),
                ((1, 512), BF16),
                ((4, 128, 1024), BF16),
                ((1024, 1024), BF16),
                ((512, 512), BF16),
                ((512, 1024), F32),
                ((512, 128), F32),
                ((1024, 512), BF16),
                ((32, 1024), F32),
                ((512, 1024), BF16),
                ((8, 8, 128), F32),
                ((16, 32, 1024), BF16),
                ((16, 32, 1024), BF16),
                ((16, 32, 1024), F32),
                *[((3, 4, 32, 512), BF16)] * 4,
                *[((4, 32, 512), F32)] * 2,
                *[((3, 32, 512), BF16)] * 4,
                ((8, 32, 128), F32),
                ((8, 32, 128), BF16),
                ((7, 32, 128), BF16),
                ((8, 32, 128), F32),
                ((2, 8, 128), F32),
                ((4, 8, 128), F32),
                ((4, 8, 128), F32),
                ((8, 8, 128), F32),
            ),
            pltpu.SemaphoreType.DMA((160,)),
            pltpu.SemaphoreType.DMA((160,)),
            pltpu.SemaphoreType.DMA((24,)),
        ],
        compiler_params=pltpu.CompilerParams(
            collective_id=0, has_side_effects=True, vmem_limit_bytes=63 * 2**20
        ),
        name="distillation_backward",
    )(
        offer_attribute_matrix, kept_offers, expert_target, sequence_extent.reshape(1, 4),
        inner_projection_matrix, v_row, behaviour_sequence,
        asking_matrix[0], lookup_matrix[0], content_matrix[0], expert_rating_vector,
    )
    return grad_hidden, grad_score.reshape(1024)


def solution(mesh):
    torus = Mesh(mesh.devices.reshape(mesh.shape["group"], NX, NY, 2), GROUP_SHARD)
    return jax.shard_map(
        body,
        mesh=torus,
        in_specs=(
            P(GROUP_SHARD, None, None),
            P(GROUP_SHARD, None),
            P(GROUP_SHARD, None),
            P(GROUP_SHARD),
            P(GROUP_SHARD, None, None),
            P(),
            P(),
            P(SHARD, None, None),
            P(SHARD, None, None),
            P(SHARD, None, None),
            P(SHARD, None),
        ),
        out_specs=(P(SHARD, None), P()),
        check_vma=False,
    )
```

```python
import functools

import jax
import jax.numpy as jnp
from jax import lax
from jax.experimental import pallas as pl
from jax.experimental.pallas import tpu as pltpu
from jax.sharding import Mesh
from jax.sharding import PartitionSpec as P

MESH = pl.DeviceIdType.MESH
F32 = jnp.float32
BF16 = jnp.bfloat16
HEADS = 8
GZ, GX, GY, GC = "group", "shard_0", "shard_1", "shard_2"
SHARD = (GX, GY, GC)
GROUP_SHARD = (GZ, GX, GY, GC)
NX, NY, NZ = 4, 4, 8
SLICE = 80
SPLIT = SLICE * NZ
NT = (((1,), (1,)), ((), ()))
TN = (((0,), (0,)), ((), ()))


def dot(a, b, dims=(((1,), (0,)), ((), ()))):
    return lax.dot_general(a, b, dims, preferred_element_type=F32)


class Sent:
    def __init__(self, copy):
        self.copy, self.arrived = copy, False
        copy.start()

    def wait_recv(self):
        if not self.arrived:
            self.copy.wait_recv()
        self.arrived = True

    def wait_send(self):
        self.copy.wait_send()


def at(axis, step, size):
    return {axis: lax.rem(lax.axis_index(axis) + (step % size), size)}


def whole_kernel(
    x_ref, kept_in, target_in, extent_in, w1_ref, v_in, hist_ref, wq_ref, wk_ref, wv_ref, rat_in,
    gh_ref, gs_ref,
    sel0, sel1, sel2, sel3, hist0, hist1, hist2, hist3,
    meta_all, meta_s, wq_all, wk_all, wr_all, wide_v, acc_v,
    kept_ref, target_ref, extent_ref, v_rows, v_ref, rat_ref,
    x_v, w1_v, wv_v, hid_v, st_v, xt_v, sum_v,
    hg_v, t_v, ga_s, ga_r, own_v, b1_s, b1_r, b2_s, b2_r, a1_v, a2_v,
    c1_s, c1_r, c2_s, c2_r, fin_v, d_s, d_r, e_v, s0_v, sx_v, sy_v, sz_v, send_sem, recv_sem, load_sem,
):
    sel_p, hist_p = (sel0, sel1, sel2, sel3), (hist0, hist1, hist2, hist3)
    x, y, z, c = (lax.axis_index(a) for a in (GX, GY, GZ, GC))
    other = {GC: 1 - c}
    used = []

    def send(src, dst, device):
        k = len(used)
        used.append(
            Sent(
                pltpu.make_async_remote_copy(
                    src_ref=src, dst_ref=dst, send_sem=send_sem.at[k], recv_sem=recv_sem.at[k],
                    device_id=device, device_id_type=MESH,
                )
            )
        )
        return used[-1]

    loads = []

    def load(src, dst):
        copy = pltpu.make_async_copy(src, dst, load_sem.at[len(loads)])
        copy.start()
        loads.append(copy)
        return copy

    xs = [at(GX, k, NX) for k in (1, 2, 3)]
    ys = [at(GY, k, NY) for k in (1, 2, 3)]
    zs = [at(GZ, k, NZ) for k in range(1, NZ)]
    diag = [{**d, **other} for d in xs]
    peers = [*xs, *ys, *zs, *diag, other]
    barrier = pltpu.get_barrier_semaphore()
    for peer in peers:
        pl.semaphore_signal(barrier, inc=1, device_id=peer, device_id_type=MESH)
    load_small = [
        load(src, dst)
        for src, dst in (
            (target_in, target_ref), (extent_in, extent_ref), (kept_in, kept_ref), (rat_in, rat_ref),
            (v_in, v_rows),
        )
    ]
    load_x = load(x_ref, x_v)
    load_wv = load(wv_ref, wv_v)
    load_own = [load(hist_ref, hist0.at[0]), load(wq_ref, wq_all.at[0]), load(wk_ref, wk_all.at[0])]
    load_w1 = load(w1_ref, w1_v)
    pl.semaphore_wait(barrier, len(peers))

    def zrows(step, start=0, size=SLICE):
        plane = lax.rem(z + (step % NZ), NZ)
        return pl.ds(pl.multiple_of(plane * SLICE + start, 16), size)

    half = SLICE // 32 * 16
    more = SLICE - half
    tail = (1024 - SPLIT) // 2
    xR, xL, yR, yL, zR, zL = xs[0], xs[2], ys[0], ys[2], zs[0], zs[6]

    zsR = send(wq_ref.at[zrows(0)], wq_all.at[2, zrows(0)], yR)
    zsL = send(wq_ref.at[zrows(0)], wq_all.at[1, zrows(0)], yL)

    def two(h):
        return pl.ds(2 * h, 2)

    def x_hist(h, device, slot):
        return send(hist_ref.at[two(h)], hist_p[slot].at[0, two(h)], device)

    def x_sel(h, device, slot):
        return send(sel0.at[0, two(h)], sel_p[slot].at[0, two(h)], device)

    def y_k(h, device, slot):
        rows = pl.ds(256 * h, 256)
        return send(wk_ref.at[rows], wk_all.at[slot, rows], device)

    def y_q(h, device, slot):
        rows = pl.ds(SPLIT + tail * h, tail)
        return send(wq_ref.at[rows], wq_all.at[slot, rows], device)

    histR, histL = {0: x_hist(0, xR, 2)}, {1: x_hist(1, xL, 1)}
    ykR, ykL = {0: y_k(0, yR, 2)}, {1: y_k(1, yL, 1)}
    for copy in load_small:
        copy.wait()
    bits = jnp.sum(jnp.left_shift(jnp.int32(1), target_ref[...]), axis=1, keepdims=True)
    meta_all[0, 0] = jnp.zeros((8, 128), jnp.int32)
    meta_all[0, 0, pl.ds(0, 4), :] = jnp.broadcast_to(bits, (4, 128))
    meta_all[0, 0, pl.ds(4, 1), pl.ds(0, 4)] = extent_ref[...]
    metaR = send(meta_all.at[0, 0], meta_all.at[2, 0], xR)
    metaL = send(meta_all.at[0, 0], meta_all.at[1, 0], xL)
    meta2 = send(meta_all.at[0, 0], meta_all.at[3, 0], xs[1])
    meta_on = [send(meta_all.at[0, 0], meta_all.at[0, 1], other)]

    for k in range(8):
        v_ref[:, pl.ds(128 * k, 128)] = v_rows[...].astype(F32)[k : k + 1, :]

    load_x.wait()
    for r in range(4):
        onehot = (
            lax.broadcasted_iota(jnp.int32, (128, 32), 0) == kept_ref[pl.ds(r, 1), :]
        ).astype(F32).astype(BF16)
        sel0[0, r] = dot(onehot, x_v[r], TN).astype(BF16)
    selR, selL = {0: x_sel(0, xR, 2)}, {1: x_sel(1, xL, 1)}

    load_wv.wait()
    head_wide = lax.broadcasted_iota(jnp.int32, (16, 512), 1) // 64
    row_of = lax.broadcasted_iota(jnp.int32, (16, 512), 0)
    rating = jnp.where(head_wide == row_of, rat_ref[...].astype(F32), 0.0).astype(BF16)
    wr_all[0] = dot(rating, wv_v[...], NT).astype(BF16)
    wrR = send(wr_all.at[0], wr_all.at[2], yR)
    wrL = send(wr_all.at[0], wr_all.at[1], yL)
    wr2 = send(wr_all.at[0], wr_all.at[3], ys[1])

    zsR.wait_recv()
    zsL.wait_recv()
    gA, gB = pl.ds(1, 2), pl.ds(3, 1)

    def z_send(group, step, device, start=0, size=SLICE):
        rows = zrows(step, start, size)
        return send(wq_all.at[group, rows], wq_all.at[group, rows], device)

    aR, aL = [z_send(gA, 0, zR)], [z_send(gA, 0, zL)]
    zs2R = send(wq_all.at[2, zrows(0, 0, half)], wq_all.at[3, zrows(0, 0, half)], yR)
    zs2L = send(wq_all.at[1, zrows(0, half, more)], wq_all.at[3, zrows(0, half, more)], yL)
    yqR, yqL = {0: y_q(0, yR, 2)}, {1: y_q(1, yL, 1)}
    histR[1], histL[0] = x_hist(1, xR, 2), x_hist(0, xL, 1)
    selR[1], selL[0] = x_sel(1, xR, 2), x_sel(0, xL, 1)
    ykR[1], ykL[0] = y_k(1, yR, 2), y_k(0, yL, 1)
    yqR[1], yqL[0] = y_q(1, yR, 2), y_q(0, yL, 1)
    on = {0: [send(hist_ref, hist0.at[1], other), send(sel0.at[0], sel0.at[1], other)], 1: [], 2: [], 3: []}

    def tower(r):
        rows = pl.ds(128 * r, 128)
        block = x_v[r]
        scores = jnp.zeros((128, 1), F32)
        for q in range(4):
            cols = pl.ds(256 * q, 256)
            hidden = jnp.maximum(dot(block, w1_v[:, cols]), 0.0)
            hid_v[rows, cols] = hidden
            scores = scores + jnp.sum(hidden * v_ref[:, cols], axis=1, keepdims=True)
        weights = jnp.exp(scores)
        st_v[rows, :] = jnp.broadcast_to(weights / jnp.sum(weights, axis=0, keepdims=True), (128, 128))
        xt_v[:, rows] = block.T

    load_w1.wait()
    tower(0)

    def x_across(refs, slot, h, arrived):
        arrived.wait_recv()
        on[slot].append(send(refs[slot].at[0, two(h)], refs[slot].at[1, two(h)], other))

    def x_forward(refs, h, arrived):
        arrived.wait_recv()
        device, slot = (xR, 2) if h == 0 else (xL, 1)
        sent = send(refs[slot].at[0, two(h)], refs[3].at[0, two(h)], device)
        x_across(refs, slot, h, arrived)
        return sent

    def y_forward(h, ak, aq):
        device, slot = (yR, 2) if h == 0 else (yL, 1)
        ak.wait_recv()
        rows = pl.ds(256 * h, 256)
        send(wk_all.at[slot, rows], wk_all.at[3, rows], device)
        aq.wait_recv()
        rows = pl.ds(SPLIT + tail * h, tail)
        send(wq_all.at[slot, rows], wq_all.at[3, rows], device)

    metaR.wait_recv()
    metaL.wait_recv()
    meta_on.append(send(meta_all.at[2, 0], meta_all.at[2, 1], other))
    meta_on.append(send(meta_all.at[1, 0], meta_all.at[1, 1], other))
    zs2R.wait_recv()
    zs2L.wait_recv()
    bR, bL = [z_send(gB, 0, zR)], [z_send(gB, 0, zL)]
    meta2.wait_recv()
    meta_on.append(send(meta_all.at[3, 0], meta_all.at[3, 1], other))

    def z_step(group, rights, lefts, k):
        cut = k == 3
        rights[k - 1].wait_recv()
        rights.append(z_send(group, -k, zR, 0, half if cut else SLICE))
        lefts[k - 1].wait_recv()
        lefts.append(z_send(group, k, zL, half if cut else 0, more if cut else SLICE))

    tower(1)
    z_step(gA, aR, aL, 1)
    tower(2)
    z_step(gB, bR, bL, 1)
    tower(3)
    for copy in meta_on:
        copy.wait_recv()
    info = [
        load(meta_all.at[k // 2, k % 2], meta_s.at[pl.ds(8 * k, 8)]) for k in range(8)
    ]
    acc_v[...] = jnp.zeros_like(acc_v)

    head_of = lax.broadcasted_iota(jnp.int32, (32, 512), 1) // 64
    slot_row = lax.broadcasted_iota(jnp.int32, (128, 256), 0)
    out_row = lax.broadcasted_iota(jnp.int32, (8, 128), 0)

    def ranked(d, p):
        step = jnp.where(d == 3, 2, jnp.where(d == 2, 3, jnp.where(d == 1, 1, 0)))
        expert = (x * 4 + lax.rem(y + step, 4)) * 2 + c
        places = []
        for core in range(2):
            base = 16 * p + 8 * core
            seen = jnp.int32(0)
            ids, found = [jnp.int32(0)] * 2, [jnp.int32(0)] * 2
            for i in range(4):
                here = lax.shift_right_logical(meta_s[base + i, 0], expert) & 1
                for j in range(2):
                    hit = jnp.where(seen == j, here, 0)
                    ids[j] = ids[j] + i * hit
                    found[j] = found[j] + hit
                seen = seen + here
            places += [(core, ids[j], found[j]) for j in range(2)]
        rows = jnp.concatenate([sel_p[p][core, i] for core, i, _ in places], axis=0)
        queries = dot(rows, wq_all[d]).astype(BF16)
        slots = jnp.concatenate([hist_p[p][core, i] for core, i, _ in places], axis=0)
        keys = dot(slots, wk_all[d]).astype(BF16)
        worth = dot(slots, wide_v[d])
        for k, (core, i, found) in enumerate(places):
            length = meta_s[16 * p + 8 * core + 4, i]
            mine = queries[32 * k : 32 * k + 32]
            spread = jnp.concatenate(
                [jnp.where(head_of == h, mine, jnp.zeros_like(mine)) for h in range(HEADS)], axis=0
            )
            logits = dot(keys[128 * k : 128 * k + 128], spread, NT) * 0.125
            w = jnp.where(slot_row < length, jnp.exp(logits), 0.0)
            top = jnp.sum(w * worth[128 * k : 128 * k + 128], axis=0, keepdims=True)
            score = top / jnp.sum(w, axis=0, keepdims=True)
            score = score[:, :128] + score[:, 128:]
            score = score + pltpu.roll(score, 64, 1)
            score = score + pltpu.roll(score, 32, 1)
            mark = out_row == jnp.where(found == 1, i, -1)
            acc_v[p, core] = acc_v[p, core] + jnp.where(mark, score, 0.0)

    def widened(d):
        small = wr_all[d].astype(F32)
        wide = [jnp.broadcast_to(small[h : h + 1, :], (32, 512)) for h in range(HEADS)]
        wide_v[d] = jnp.concatenate(wide, axis=0).T.astype(BF16)

    def expert_run(low, high, groups):
        @pl.loop(low, high)
        def _(d):
            for p in groups:
                ranked(d, p)

    def arrived(*copies):
        for copy in copies:
            copy.wait_recv()

    for copy in (*info, *load_own):
        copy.wait()
    widened(0)
    arrived(*on[0])
    ranked(0, 0)
    z_step(gA, aR, aL, 2)
    arrived(wrR, wrL, wr2)

    @pl.loop(1, 4)
    def _(d):
        widened(d)

    hist2R = x_forward(hist_p, 0, histR[0])
    hist2L = x_forward(hist_p, 1, histL[1])
    sel2R = x_forward(sel_p, 0, selR[0])
    sel2L = x_forward(sel_p, 1, selL[1])
    y_forward(0, ykR[0], yqR[0])
    y_forward(1, ykL[1], yqL[1])
    z_step(gB, bR, bL, 2)
    z_step(gA, aR, aL, 3)
    x_across(hist_p, 2, 1, histR[1])
    x_across(hist_p, 1, 0, histL[0])
    x_across(sel_p, 2, 1, selR[1])
    x_across(sel_p, 1, 0, selL[0])
    arrived(*on[1], *on[2])
    ranked(0, 1)
    ranked(0, 2)
    z_step(gB, bR, bL, 3)
    x_across(hist_p, 3, 0, hist2R)
    x_across(hist_p, 3, 1, hist2L)
    x_across(sel_p, 3, 0, sel2R)
    x_across(sel_p, 3, 1, sel2L)
    arrived(*ykR.values(), *ykL.values(), *yqR.values(), *yqL.values(), *aR, *aL)
    expert_run(1, 3, range(3))
    arrived(*on[3])
    expert_run(0, 3, (3,))
    arrived(*used)
    back = []
    for p, k in ((3, 2), (1, 1), (2, 3), (0, 0)):
        ranked(3, p)
        if k:
            back.append(send(acc_v.at[p, 0], t_v.at[2 * p], xs[k - 1]))
        back.append(send(acc_v.at[p, 1], t_v.at[2 * p + 1], diag[k - 1] if k else other))
    t_v[0] = acc_v[0, 0]
    for copy in back:
        copy.wait_recv()
    teacher = t_v[0]
    for k in range(1, 8):
        teacher = teacher + t_v[k]
    live = lax.broadcasted_iota(jnp.int32, (8, 128), 1) < 32
    risen = jnp.where(live, jnp.exp(teacher / 6.0), 0.0)
    t_v[0] = risen / jnp.sum(risen, axis=1, keepdims=True)

    for r in range(4):
        rows = pl.ds(128 * r, 128)
        spots = lax.broadcasted_iota(jnp.int32, (128, 32), 0) == kept_ref[pl.ds(r, 1), :]
        aim = jnp.sum(jnp.where(spots, t_v[0, pl.ds(r, 1), pl.ds(0, 32)], 0.0), axis=1, keepdims=True)
        grad = st_v[rows, pl.ds(0, 1)] - aim
        for q in range(4):
            cols = pl.ds(256 * q, 256)
            hidden = hid_v[rows, cols]
            hg_v[rows, cols] = jnp.where(hidden > 0.0, grad * v_ref[:, cols], 0.0).astype(BF16)
            sum_v[pl.ds(8 * r, 8), cols] = jnp.sum((grad * hidden).reshape(16, 8, 256), axis=0)
    row = jnp.sum(sum_v[...], axis=0, keepdims=True)
    for k in range(8):
        s0_v[0, pl.ds(k, 1), :] = row[:, 128 * k : 128 * k + 128]
    sa = send(s0_v.at[0], s0_v.at[1], other)

    core = []

    def rows_of(k, side):
        return jnp.concatenate(
            [xt_v[pl.ds(pl.multiple_of(64 * (4 * k + j) + 32 * side, 32), 32), :] for j in range(4)], axis=0
        )

    n1, n2 = pl.ds(0, 512), pl.ds(512, 512)

    def along_x(side, h):
        return own_v[pl.ds(4 * side[GX] + 2 * h, 2), :, n1]

    def along_y(side, h):
        return jnp.stack([own_v[4 * (2 * h + j) + side[GY], :, n2] for j in range(2)])

    ways = ((along_x, xs, b1_s, b1_r), (along_y, ys, b2_s, b2_r))
    relay, direct = [], []

    def to_relay(part, sides, out, into):
        for h, device in ((0, sides[0]), (1, sides[2])):
            out[0, pl.ds(2 * h, 2)] = part(sides[1], h).astype(BF16)
            relay.append(send(out.at[0, pl.ds(2 * h, 2)], into.at[0, pl.ds(2 * h, 2)], device))

    def to_next(part, sides, out, into, h):
        k, device = 2 - h, sides[0] if h == 1 else sides[2]
        out[k, pl.ds(2 * h, 2)] = part(device, h).astype(BF16)
        direct.append(send(out.at[k, pl.ds(2 * h, 2)], into.at[k, pl.ds(2 * h, 2)], device))

    order = [xs[1][GX], xs[0][GX], xs[2][GX], x]
    for k in range(4):
        blocks = pl.ds(4 * order[k], 4)
        ga_s[blocks] = dot(rows_of(order[k], 1 - c), hg_v[...]).astype(BF16).reshape(4, 32, 1024)
        core.append(send(ga_s.at[blocks], ga_r.at[blocks], other))
    for k in range(4):
        own_v[pl.ds(4 * order[k], 4)] = dot(rows_of(order[k], c), hg_v[...]).reshape(4, 32, 1024)
    for k in range(4):
        core[k].wait_recv()
        blocks = pl.ds(4 * order[k], 4)
        own_v[blocks] = own_v[blocks] + ga_r[blocks].astype(F32)
        if k == 0:
            to_relay(*ways[0])
        if k in (1, 2):
            to_next(*ways[0], 2 - k)
    to_relay(*ways[1])
    to_next(*ways[1], 1)
    to_next(*ways[1], 0)
    sa.wait_recv()
    sx_v[x] = s0_v[0] + s0_v[1]
    sb = [send(sx_v.at[x], sx_v.at[x], xs[k]) for k in range(3)]
    for n, (part, sides, out, into) in enumerate(ways):
        for h, device in ((0, sides[0]), (1, sides[2])):
            relay[2 * n + h].wait_recv()
            k = 1 + h
            rows = pl.ds(2 * h, 2)
            out[k, rows] = (part(device, h) + into[0, rows].astype(F32)).astype(BF16)
            direct.append(send(out.at[k, rows], into.at[k, rows], device))
    for copy in sb:
        copy.wait_recv()
    sy_v[y] = (sx_v[0] + sx_v[1]) + (sx_v[2] + sx_v[3])
    sc = [send(sy_v.at[y], sy_v.at[y], ys[k]) for k in range(3)]
    for copy in direct:
        copy.wait_recv()
    a1_v[...] = own_v[pl.ds(4 * x, 4), :, n1] + (b1_r[1].astype(F32) + b1_r[2].astype(F32))
    for j in range(4):
        a2_v[j] = own_v[4 * j + y, :, n2] + (b2_r[1, j].astype(F32) + b2_r[2, j].astype(F32))
    third = []
    for k in (2, 1, 3):
        c1_s[k - 1] = a1_v[ys[k - 1][GY]].astype(BF16)
        third.append(send(c1_s.at[k - 1], c1_r.at[k - 1], ys[k - 1]))
    for k in (2, 1, 3):
        c2_s[k - 1] = a2_v[xs[k - 1][GX]].astype(BF16)
        third.append(send(c2_s.at[k - 1], c2_r.at[k - 1], xs[k - 1]))
    for copy in sc:
        copy.wait_recv()
    sz_v[z] = (sy_v[0] + sy_v[1]) + (sy_v[2] + sy_v[3])
    sd = [send(sz_v.at[z], sz_v.at[z], zs[k]) for k in range(NZ - 1)]
    for copy in third:
        copy.wait_recv()
    fin1 = a1_v[y] + (c1_r[0].astype(F32) + c1_r[1].astype(F32) + c1_r[2].astype(F32))
    fin2 = a2_v[x] + (c2_r[0].astype(F32) + c2_r[1].astype(F32) + c2_r[2].astype(F32))
    for k in range(4):
        fin_v[k] = fin1[:, 128 * k : 128 * k + 128]
        fin_v[4 + k] = fin2[:, 128 * k : 128 * k + 128]
    d_s[...] = fin_v[...].astype(BF16)

    fourth = []
    for k in (4, 3, 5, 2, 6, 1, 7):
        fourth.append(send(d_s.at[zs[k - 1][GZ]], d_r.at[k - 1], zs[k - 1]))
    for copy in fourth:
        copy.wait_recv()
    whole = fin_v[z]
    for k in range(NZ - 1):
        whole = whole + d_r[k].astype(F32)
    e_v[z] = whole
    fifth = [send(e_v.at[z], e_v.at[z], zs[k - 1]) for k in (4, 3, 5, 2, 6, 1, 7)]
    for copy in sd:
        copy.wait_recv()
    gs = sz_v[0]
    for k in range(1, NZ):
        gs = gs + sz_v[k]
    gs_ref[...] = gs
    for copy in fifth:
        copy.wait_recv()
    for k in range(NZ):
        gh_ref[:, pl.ds(128 * k, 128)] = e_v[k]
    for copy in used:
        copy.wait_send()


def vmem(*items):
    return [pltpu.VMEM(s, t) for s, t in items]


def body(
    offer_attribute_matrix,
    kept_offers,
    expert_target,
    sequence_extent,
    behaviour_sequence,
    inner_projection_matrix,
    student_rating_vector,
    asking_matrix,
    lookup_matrix,
    content_matrix,
    expert_rating_vector,
):
    v_row = student_rating_vector.reshape(8, 128)
    grad_hidden, grad_score = pl.pallas_call(
        whole_kernel,
        out_shape=[jax.ShapeDtypeStruct((32, 1024), F32), jax.ShapeDtypeStruct((8, 128), F32)],
        in_specs=[pl.BlockSpec(memory_space=pl.ANY)] * 11,
        out_specs=[pl.BlockSpec(memory_space=pltpu.VMEM)] * 2,
        scratch_shapes=[
            *vmem(*[((2, 4, 32, 1024), BF16)] * 4, *[((2, 4, 128, 512), BF16)] * 4),
            pltpu.VMEM((4, 2, 8, 128), jnp.int32),
            pltpu.SMEM((64, 128), jnp.int32),
            *vmem(
                ((4, 1024, 512), BF16),
                ((4, 512, 512), BF16),
                ((4, 16, 512), BF16),
                ((4, 512, 256), BF16),
                ((4, 2, 8, 128), F32),
                ((4, 32), jnp.int32),
                ((4, 6), jnp.int32),
                ((1, 4), jnp.int32),
                ((8, 128), BF16),
                ((1, 1024), F32),
                ((1, 512), BF16),
                ((4, 128, 1024), BF16),
                ((1024, 1024), BF16),
                ((512, 512), BF16),
                ((512, 1024), F32),
                ((512, 128), F32),
                ((1024, 512), BF16),
                ((32, 1024), F32),
                ((512, 1024), BF16),
                ((8, 8, 128), F32),
                ((16, 32, 1024), BF16),
                ((16, 32, 1024), BF16),
                ((16, 32, 1024), F32),
                *[((3, 4, 32, 512), BF16)] * 4,
                *[((4, 32, 512), F32)] * 2,
                *[((3, 32, 512), BF16)] * 4,
                ((8, 32, 128), F32),
                ((8, 32, 128), BF16),
                ((7, 32, 128), BF16),
                ((8, 32, 128), F32),
                ((2, 8, 128), F32),
                ((4, 8, 128), F32),
                ((4, 8, 128), F32),
                ((8, 8, 128), F32),
            ),
            pltpu.SemaphoreType.DMA((160,)),
            pltpu.SemaphoreType.DMA((160,)),
            pltpu.SemaphoreType.DMA((24,)),
        ],
        compiler_params=pltpu.CompilerParams(
            collective_id=0, has_side_effects=True, vmem_limit_bytes=63 * 2**20
        ),
        name="distillation_backward",
    )(
        offer_attribute_matrix, kept_offers, expert_target, sequence_extent.reshape(1, 4),
        inner_projection_matrix, v_row, behaviour_sequence,
        asking_matrix[0], lookup_matrix[0], content_matrix[0], expert_rating_vector,
    )
    return grad_hidden, grad_score.reshape(1024)


def solution(mesh):
    torus = Mesh(mesh.devices.reshape(mesh.shape["group"], NX, NY, 2), GROUP_SHARD)
    return jax.shard_map(
        body,
        mesh=torus,
        in_specs=(
            P(GROUP_SHARD, None, None),
            P(GROUP_SHARD, None),
            P(GROUP_SHARD, None),
            P(GROUP_SHARD),
            P(GROUP_SHARD, None, None),
            P(),
            P(),
            P(SHARD, None, None),
            P(SHARD, None, None),
            P(SHARD, None, None),
            P(SHARD, None),
        ),
        out_specs=(P(SHARD, None), P()),
        check_vma=False,
    )
```
